512 devices in a mesh: dp: 16 (over x, y_lo), mp: 32 (over y_hi, z, core).
Axes of the slice: x: 4, y: 8 (y_hi: 2, y_lo: 4; y = y_hi * 4 + y_lo), z: 8, core: 2. Of those that a mesh axis runs over, the one named last changes fastest.
Arguments:
- block_input: bfloat16 [2048, 6144], P('mp', 'dp'), may hold values from -64 to 64
- ln_gain: float32 [6144], P('dp'), may hold values from 0.5 to 1.5
- w_qkv: bfloat16 [6144, 12288], P('dp', 'mp'), may hold values from -0.078125 to 0.078125
- w_in: bfloat16 [6144, 12288], P('dp', 'mp'), may hold values from -0.078125 to 0.078125
- w_o: bfloat16 [4096, 6144], P('mp', 'dp'), may hold values from -0.09375 to 0.09375
- w_out: bfloat16 [12288, 6144], P('mp', 'dp'), may hold values from -0.0546875 to 0.0546875
- q_gain: float32 [32, 128], P('mp'), may hold values from 0.5 to 1.5
- k_gain: float32 [32, 128], P('mp'), may hold values from 0.5 to 1.5
- cotangent: bfloat16 [2048, 6144], P('mp', 'dp'), may hold values from -3 to 3
Outputs:
- output: bfloat16 [2048, 6144], P('mp', 'dp')
- grad_x: bfloat16 [2048, 6144], P('mp', 'dp')
- grad_w_qkv: bfloat16 [6144, 12288], P('dp', 'mp')
- grad_w_in: bfloat16 [6144, 12288], P('dp', 'mp')
- grad_w_o: bfloat16 [4096, 6144], P('mp', 'dp')
- grad_w_out: bfloat16 [12288, 6144], P('mp', 'dp')
The draws below stay inside these ranges and needn't reach their ends.
All inputs are finite; a program needn't handle non-finite values.
Results may differ from the reference program's by a relative error of at most 0.038.
Values may be sent and summed in bfloat16 or wider, within the bound.
A program may use at most 64 MiB of HBM per device.

```python
import math
import jax
import jax.numpy as jnp
from jax import lax

D = 6144
HD = 128
HEAD_DEV = 1
FF_DEV = 384
PATCH = 128
HEADS = 32
FF = 12288
TOKENS = 2048
N_DP = 16
N_MP = 32


def draw_block_input(key, part):
    key = jax.random.fold_in(key, 11)
    keys = jax.random.split(key, 4)
    position = jnp.arange(D, dtype=jnp.float32) / D
    rising = jnp.exp(jnp.log(3.0) * (position - 0.5))
    col_scale = jnp.exp(jax.random.uniform(keys[0], (1, D), minval=jnp.log(0.3), maxval=jnp.log(3.0))) * rising
    row_scale = jnp.exp(jax.random.uniform(keys[1], (TOKENS, 1), minval=jnp.log(0.3), maxval=jnp.log(3.0)))
    base = jax.random.truncated_normal(keys[3], -4.0, 4.0, (TOKENS, D))
    return (base * row_scale * col_scale).astype(jnp.bfloat16)


def level_of(stream_key, extent, cuts, low, top_value):
    def one(axis_at, shards_of):
        draws = jax.random.uniform(jax.random.fold_in(jax.random.fold_in(stream_key, 6), axis_at), (shards_of,), jnp.float32, low / len(cuts), top_value / len(cuts))
        return jnp.repeat(jnp.exp(draws), extent[axis_at] // shards_of).reshape((-1,) + (1,) * (len(extent) - axis_at - 1))

    factor_of = one(*cuts[0])
    for cut in cuts[1:]:
        factor_of = factor_of * one(*cut)
    return factor_of


def noise(rng, shape, deviation, reach, pieces=(), held_as=jnp.bfloat16):
    entries = jax.random.normal(rng, shape, jnp.float32) * deviation
    if len(pieces) > 0:
        entries = level_of(rng, shape, pieces, -0.22, 0.18) * entries
    return jnp.clip(entries, min=-reach, max=reach).astype(held_as)


def setup_inputs(seed: int = 0) -> dict:
    splits = jax.random.split(jax.random.key(seed), 10)
    return {
        "block_input": draw_block_input(jax.random.fold_in(splits[9], 71), 0),
        "ln_gain": jnp.clip(1.0 + 0.1 * jax.random.normal(splits[1], (D,), jnp.float32), 0.5, 1.5),
        "w_qkv": noise(splits[2], (D, 3 * HEADS * HD), D ** -0.5, 0.078125, ((0, 16), (1, 32))),
        "w_in": noise(splits[3], (D, FF), D ** -0.5, 0.078125, ((0, 16), (1, 32))),
        "w_o": noise(splits[4], (HEADS * HD, D), (HEADS * HD) ** -0.5, 0.09375, ((0, 32), (1, 16))),
        "w_out": noise(splits[5], (FF, D), FF ** -0.5, 0.0546875, ((0, 32), (1, 16))),
        "q_gain": jnp.clip(1.0 + 0.1 * jax.random.normal(splits[6], (HEADS, HD), jnp.float32), 0.5, 1.5),
        "k_gain": jnp.clip(1.0 + 0.1 * jax.random.normal(splits[7], (HEADS, HD), jnp.float32), 0.5, 1.5),
        "cotangent": noise(splits[8], (TOKENS, D), 0.5, 3.0, ((0, 32), (1, 16))),
    }


epsilon = 1e-06

def block_product(left, right, blocks):
    inner = left.shape[1] // blocks

    def accumulate(total, which):
        left_piece = lax.dynamic_slice_in_dim(left, which * inner, inner, 1)
        right_piece = lax.dynamic_slice_in_dim(right, which * inner, inner, 0)
        partial_sum = jnp.dot(left_piece, right_piece, preferred_element_type=jnp.float32).astype(jnp.bfloat16)
        partial_sum = lax.optimization_barrier(partial_sum)
        return (total + partial_sum.astype(jnp.float32), None)
    start_total = jnp.zeros((left.shape[0], right.shape[1]), jnp.float32)
    total, _ = lax.scan(accumulate, start_total, jnp.arange(blocks, dtype=jnp.int32))
    return total

def head_norm(values, gain):
    centre = values - lax.optimization_barrier(jnp.mean(values, -1, keepdims=True))
    scaling = 1.0 / jnp.sqrt(lax.optimization_barrier(jnp.mean(centre * centre, -1, keepdims=True)) + epsilon)
    unit = centre * scaling
    return (unit * gain, unit, scaling)

def head_back(grad, unit, scaling, gain):
    local_grad = grad * gain
    return scaling * (local_grad - lax.optimization_barrier(jnp.mean(local_grad, -1, keepdims=True)) - unit * lax.optimization_barrier(jnp.mean(local_grad * unit, -1, keepdims=True)))

def gelu_tanh(values):
    return jax.nn.gelu(values, approximate=True)

def reference(block_input, ln_gain, w_qkv, w_in, w_o, w_out, q_gain, k_gain, cotangent):
    inputs = block_input.astype(jnp.float32)
    mean = lax.optimization_barrier(jnp.sum(inputs, 1, keepdims=True)) / D
    centred_raw = inputs - mean
    spread = lax.optimization_barrier(jnp.sum(centred_raw * centred_raw, 1, keepdims=True)) / D
    scaling = 1.0 / jnp.sqrt(spread + epsilon)
    centred = centred_raw * scaling
    normed = (centred * ln_gain).astype(jnp.bfloat16)
    qkv = block_product(normed, w_qkv, N_DP)
    pre = block_product(normed, w_in, N_DP)
    images = TOKENS // PATCH
    triples = qkv.reshape(images, PATCH, HEADS, 3, HD)
    queries, query_unit, query_scale = head_norm(triples[:, :, :, 0], q_gain)
    keys_normed, key_unit, key_scale = head_norm(triples[:, :, :, 1], k_gain)
    query_b = queries.astype(jnp.bfloat16).astype(jnp.float32)
    key_b = keys_normed.astype(jnp.bfloat16).astype(jnp.float32)
    value_b = triples[:, :, :, 2].astype(jnp.bfloat16).astype(jnp.float32)
    factor = 1.0 / math.sqrt(HD)
    scores = jnp.einsum('iphd,iqhd->ihpq', query_b, key_b) * factor
    expo = jnp.exp(scores)
    prob = expo / lax.optimization_barrier(jnp.sum(expo, -1, keepdims=True))
    prob_b = prob.astype(jnp.bfloat16).astype(jnp.float32)
    attended = jnp.einsum('ihpq,iqhd->iphd', prob_b, value_b).astype(jnp.bfloat16).reshape(TOKENS, HEADS * HD)
    active = gelu_tanh(pre).astype(jnp.bfloat16)
    head_cols = HEAD_DEV * HD
    mixed = jnp.concatenate([attended.reshape(TOKENS, N_MP, head_cols), active.reshape(TOKENS, N_MP, FF_DEV)], 2).reshape(TOKENS, -1)
    out_weights = jnp.concatenate([w_o.reshape(N_MP, head_cols, D), w_out.reshape(N_MP, FF_DEV, D)], 1).reshape(-1, D)
    output = (inputs + block_product(mixed, out_weights, N_MP)).astype(jnp.bfloat16)
    grad_mixed = block_product(cotangent, out_weights.T, N_DP).reshape(TOKENS, N_MP, head_cols + FF_DEV)
    grad_attn = grad_mixed[:, :, :head_cols].reshape(images, PATCH, HEADS, HD).astype(jnp.bfloat16).astype(jnp.float32)
    grad_act = grad_mixed[:, :, head_cols:].reshape(TOKENS, FF)
    out_grads = jnp.dot(mixed.T, cotangent, preferred_element_type=jnp.float32).reshape(N_MP, head_cols + FF_DEV, D)
    grad_w_o = out_grads[:, :head_cols].reshape(HEADS * HD, D).astype(jnp.bfloat16)
    grad_w_out = out_grads[:, head_cols:].reshape(FF, D).astype(jnp.bfloat16)
    _, pullback = jax.vjp(gelu_tanh, pre)
    grad_pre = pullback(grad_act)[0].astype(jnp.bfloat16)
    dprob = jnp.einsum('iphd,iqhd->ihpq', grad_attn, value_b)
    delta = lax.optimization_barrier(jnp.sum(prob * dprob, -1, keepdims=True))
    dscore = (prob * (dprob - delta)).astype(jnp.bfloat16).astype(jnp.float32)
    grad_qn = jnp.einsum('ihpq,iqhd->iphd', dscore, key_b) * factor
    grad_kn = jnp.einsum('ihpq,iphd->iqhd', dscore, query_b) * factor
    grad_v = jnp.einsum('ihpq,iphd->iqhd', prob_b, grad_attn)
    grad_q = head_back(grad_qn, query_unit, query_scale, q_gain)
    grad_k = head_back(grad_kn, key_unit, key_scale, k_gain)
    grad_qkv = jnp.stack([grad_q, grad_k, grad_v], 3).reshape(TOKENS, 3 * HEADS * HD).astype(jnp.bfloat16)
    grad_w_qkv = jnp.dot(normed.T, grad_qkv, preferred_element_type=jnp.float32).astype(jnp.bfloat16)
    grad_w_in = jnp.dot(normed.T, grad_pre, preferred_element_type=jnp.float32).astype(jnp.bfloat16)
    grad_left = jnp.concatenate([grad_qkv.reshape(TOKENS, N_MP, 3 * head_cols), grad_pre.reshape(TOKENS, N_MP, FF_DEV)], 2).reshape(TOKENS, -1)
    grad_right = jnp.concatenate([w_qkv.T.reshape(N_MP, 3 * head_cols, D), w_in.T.reshape(N_MP, FF_DEV, D)], 1).reshape(-1, D)
    grad_normed = block_product(grad_left, grad_right, N_MP)
    local_grad = grad_normed * ln_gain
    first = lax.optimization_barrier(jnp.sum(local_grad, 1, keepdims=True)) / D
    second = lax.optimization_barrier(jnp.sum(local_grad * centred, 1, keepdims=True)) / D
    grad_x = (cotangent.astype(jnp.float32) + scaling * (local_grad - first - centred * second)).astype(jnp.bfloat16)
    return (output, grad_x, grad_w_qkv, grad_w_in, grad_w_o, grad_w_out)
```

```python
import math

import jax
import jax.numpy as jnp
from jax import lax
from jax.experimental import pallas as pl
from jax.experimental.pallas import tpu as pltpu
from jax.sharding import PartitionSpec as P

MESH = pl.DeviceIdType.MESH
D = 6144
FEATURES = 384
N_DP = 16
epsilon = 1e-06
F32 = jnp.float32
BF16 = jnp.bfloat16
FACTOR = 1.0 / math.sqrt(128)
GELU_ROOT = 0.7978845608028654
GELU_CUBE = 0.044715
NT = (((1,), (1,)), ((), ()))
TN = (((0,), (0,)), ((), ()))
COPIES = 200


def mm(a, b):
    return jnp.dot(a, b, preferred_element_type=F32)


def mm_nt(a, b):
    return lax.dot_general(a, b, NT, preferred_element_type=F32)


def mm_tn(a, b):
    return lax.dot_general(a, b, TN, preferred_element_type=F32)


def up(v):
    return v.astype(F32)


def head_norm(values, gain):
    centre = values - jnp.mean(values, -1, keepdims=True)
    scaling = 1.0 / jnp.sqrt(jnp.mean(centre * centre, -1, keepdims=True) + epsilon)
    unit = centre * scaling
    return (unit * gain, unit, scaling)


def head_back(grad, unit, scaling, gain):
    local_grad = grad * gain
    return scaling * (
        local_grad
        - jnp.mean(local_grad, -1, keepdims=True)
        - unit * jnp.mean(local_grad * unit, -1, keepdims=True)
    )


def columns_to_rows(first, second):
    lane = lax.broadcasted_iota(jnp.int32, (64, 128), 1)
    block = jnp.where(lane == 0, first, jnp.where(lane == 1, second, 0.0))
    block = jnp.concatenate([block, jnp.zeros((64, 128), F32)], 0)
    return block.T[:8]


def rows_to_columns(first, second):
    row = lax.broadcasted_iota(jnp.int32, (128, 128), 0)
    block = jnp.where(row == 0, first, jnp.where(row == 1, second, 0.0)).T
    return block[:64, 0:1], block[:64, 1:2]


def kernel(
    x_ref, cot_ref, gain_ref, wqkv_ref, win_ref, wo_ref, wout_ref, qg_ref, kg_ref,
    out_ref, gx_ref, gwqkv_ref, gwin_ref, gwo_ref, gwout_ref,
    cot_all, nrm_all, bw, ow, stats, stats_b, cen_ref, scl_ref,
    g1, g2, fp, rg1, rg2, rfp, s1, s2, sf, tg1, tg2, tfp,
    m_all, ra_all, rb_all, eo, eg, reo, reg, so, sg, lo, ro, lg, rg, fo, fg, yo, yg, ryo, ryg,
    send, recv,
):
    d = lax.axis_index("dp")
    m = lax.axis_index("mp")
    x, y = d // 4, lax.rem(d, 4)
    h, z, c = m // 16, lax.rem(m // 2, 8), lax.rem(m, 2)

    def dp_at(xx, yy):
        return (xx * 4 + yy, m)

    x_peers = [dp_at(lax.rem(x + o, 4), y) for o in (1, 2, 3)]
    y_peers = [dp_at(x, lax.rem(y + o, 4)) for o in (1, 2, 3)]
    dp_peers = [(lax.rem(d + o, N_DP), m) for o in range(1, N_DP)]
    hi_peer = (d, (1 - h) * 16 + z * 2 + c)
    z_right = (d, h * 16 + lax.rem(z + 1, 8) * 2 + c)
    z_left = (d, h * 16 + lax.rem(z + 7, 8) * 2 + c)
    core_peer = (d, m + 1 - 2 * c)

    barrier = pltpu.get_barrier_semaphore()
    everyone = dp_peers + [hi_peer, z_right, z_left, core_peer]
    for peer in everyone:
        pl.semaphore_signal(barrier, inc=1, device_id=peer, device_id_type=MESH)

    started = []

    def push(src, dst, peer):
        n = len(started)
        copy = pltpu.make_async_remote_copy(
            src_ref=src, dst_ref=dst, send_sem=send.at[n], recv_sem=recv.at[n],
            device_id=peer, device_id_type=MESH,
        )
        copy.start()
        started.append(copy)
        return copy

    def arrive(copies):
        for copy in copies:
            copy.wait_recv()

    mine = h * 8 + z
    cot_all[mine, c] = cot_ref[...]
    inputs = up(x_ref[...])
    local_mean = jnp.sum(inputs, 1, keepdims=True) / FEATURES
    local_centre = inputs - local_mean
    local_m2 = jnp.sum(local_centre * local_centre, 1, keepdims=True)
    stats[d] = columns_to_rows(local_mean, local_m2)
    bw[:, :384] = wqkv_ref[...]
    bw[:, 384:] = win_ref[...]
    ow[:128] = wo_ref[...]
    ow[128:] = wout_ref[...]
    pl.semaphore_wait(barrier, len(everyone))

    def hi_start(a):
        return [push(a.at[mine, c], a.at[mine, c], hi_peer)]

    def ring_start(a, kind, s):
        hh = h if kind == 0 else 1 - h
        right = hh * 8 + lax.rem(z + 9 - s, 8)
        left = hh * 8 + lax.rem(z + s - 1, 8)
        if s == 4:
            first, second = pl.ds(0, 32), pl.ds(32, 32)
            return [
                push(a.at[right, c, first], a.at[right, c, first], z_right),
                push(a.at[left, c, second], a.at[left, c, second], z_left),
            ]
        return [
            push(a.at[right, c], a.at[right, c], z_right),
            push(a.at[left, c], a.at[left, c], z_left),
        ]

    def core_start(a):
        return [push(a.at[:, c], a.at[:, c], core_peer)]

    ch = hi_start(cot_all)
    ca = ring_start(cot_all, 0, 1)
    st = [push(stats.at[d], stats.at[d], peer) for peer in dp_peers]
    arrive(ch)
    cb = ring_start(cot_all, 1, 1)
    arrive(ca)
    ca = ring_start(cot_all, 0, 2)
    arrive(st)
    every = stats[...]
    mean_row = jnp.sum(every[:, 0:1, :], 0) / N_DP
    apart = every[:, 0:1, :] - mean_row[None]
    m2_row = jnp.sum(every[:, 1:2, :], 0) + FEATURES * jnp.sum(apart * apart, 0)
    scaling_row = 1.0 / jnp.sqrt(m2_row / D + epsilon)
    mean, scaling = rows_to_columns(mean_row, scaling_row)
    centred = (inputs - mean) * scaling
    cen_ref[...] = centred
    scl_ref[...] = jnp.broadcast_to(scaling, (64, 128))
    nrm_all[mine, c] = (centred * gain_ref[...]).astype(BF16)
    nh = hi_start(nrm_all)
    na = ring_start(nrm_all, 0, 1)
    arrive(cb)
    cb = ring_start(cot_all, 1, 2)
    arrive(ca)
    ca = ring_start(cot_all, 0, 3)
    arrive(nh)
    nb = ring_start(nrm_all, 1, 1)
    arrive(na)
    na = ring_start(nrm_all, 0, 2)
    arrive(cb)
    cb = ring_start(cot_all, 1, 3)
    arrive(ca)
    ca = ring_start(cot_all, 0, 4)
    arrive(nb)
    nb = ring_start(nrm_all, 1, 2)
    arrive(na)
    na = ring_start(nrm_all, 0, 3)
    arrive(cb)
    cb = ring_start(cot_all, 1, 4)
    arrive(ca)
    arrive(cb)
    cc = core_start(cot_all)
    arrive(nb)
    nb = ring_start(nrm_all, 1, 3)
    arrive(na)
    na = ring_start(nrm_all, 0, 4)
    arrive(cc)

    for xx in range(4):
        rows = cot_all[4 * xx : 4 * xx + 4].reshape(512, FEATURES)
        product = mm_nt(rows, ow[...]).astype(BF16)
        g1[xx] = product[:, :256].reshape(4, 128, 256)
        g2[xx] = product[:, 256:].reshape(4, 128, 256)
    w1 = [
        push(g1.at[:, lax.rem(y + o, 4)], rg1.at[o - 1], y_peers[o - 1]) for o in (1, 2, 3)
    ]
    w2 = [push(g2.at[lax.rem(x + o, 4)], rg2.at[o - 1], x_peers[o - 1]) for o in (1, 2, 3)]
    arrive(nb)
    nb = ring_start(nrm_all, 1, 4)
    arrive(na)
    arrive(nb)
    arrive(core_start(nrm_all))

    wf = [[], [], [], []]
    for o in (1, 2, 3, 0):
        xx = lax.rem(x + o, 4)
        rows = nrm_all[pl.ds(4 * xx, 4)].reshape(512, FEATURES)
        fp[xx] = mm(rows, bw[...]).astype(BF16).reshape(4, 128, 768)
        if o:
            for k in range(4):
                yy = lax.rem(y + k + 1, 4)
                wf[k].append(push(fp.at[xx, yy], rfp.at[o - 1, k], x_peers[o - 1]))

    def fsum(k):
        yy = lax.rem(y + k + 1, 4)
        return up(fp[x, yy]) + up(rfp[0, k]) + up(rfp[1, k]) + up(rfp[2, k])

    tf = []
    t2 = []
    for k in range(3):
        arrive(wf[k])
        sf[k] = fsum(k).astype(BF16)
        tf.append(push(sf.at[k], tfp.at[k], y_peers[k]))
        if k == 0:
            arrive(w2)
            for j in range(3):
                yy = lax.rem(y + j + 1, 4)
                total = up(g2[x, yy]) + up(rg2[0, yy]) + up(rg2[1, yy]) + up(rg2[2, yy])
                s2[j] = total.astype(BF16)
                t2.append(push(s2.at[j], tg2.at[j], y_peers[j]))
    arrive(w1)
    t1 = []
    for j in range(3):
        xx = lax.rem(x + j + 1, 4)
        total = up(g1[xx, y]) + up(rg1[0, xx]) + up(rg1[1, xx]) + up(rg1[2, xx])
        s1[j] = total.astype(BF16)
        t1.append(push(s1.at[j], tg1.at[j], x_peers[j]))
    arrive(t2)
    gm2 = up(g2[x, y]) + up(rg2[0, y]) + up(rg2[1, y]) + up(rg2[2, y])
    gm2 = gm2 + up(tg2[0]) + up(tg2[1]) + up(tg2[2])
    arrive(wf[3])
    own_sum = fsum(3)
    arrive(tf)
    features = own_sum + up(tfp[0]) + up(tfp[1]) + up(tfp[2])
    arrive(t1)
    gm1 = up(g1[x, y]) + up(rg1[0, x]) + up(rg1[1, x]) + up(rg1[2, x])
    gm1 = gm1 + up(tg1[0]) + up(tg1[1]) + up(tg1[2])

    qg, kg = qg_ref[...], kg_ref[...]
    queries, query_unit, query_scale = head_norm(features[:, :128], qg)
    keys, key_unit, key_scale = head_norm(features[:, 128:256], kg)
    query_b, key_b = queries.astype(BF16), keys.astype(BF16)
    value_b = features[:, 256:384].astype(BF16)
    pre = features[:, 384:]
    expo = jnp.exp(mm_nt(query_b, key_b) * FACTOR)
    prob = expo / jnp.sum(expo, -1, keepdims=True)
    prob_b = prob.astype(BF16)
    inner = GELU_ROOT * (pre + GELU_CUBE * (pre * pre * pre))
    bend = jnp.tanh(inner)
    m_all[x, y, :, :128] = mm(prob_b, value_b).astype(BF16)
    m_all[x, y, :, 128:] = (0.5 * pre * (1.0 + bend)).astype(BF16)
    own_m = m_all.at[x, y]
    m_y = [push(own_m, own_m, peer) for peer in y_peers]
    m_x = [push(own_m, own_m, peer) for peer in x_peers]
    slope = 0.5 * (1.0 + bend) + 0.5 * pre * (1.0 - bend * bend) * (
        GELU_ROOT * (1.0 + 3.0 * GELU_CUBE * (pre * pre))
    )
    grad_attn = gm1[:, :128].astype(BF16)
    grad_act = jnp.concatenate([gm1[:, 128:], gm2], 1)
    rb_all[x, y, :, 128:] = (grad_act * slope).astype(BF16)
    dprob = mm_nt(grad_attn, value_b)
    delta = jnp.sum(prob * dprob, -1, keepdims=True)
    dscore = (prob * (dprob - delta)).astype(BF16)
    grad_qn = mm(dscore, key_b) * FACTOR
    grad_kn = mm_tn(dscore, query_b) * FACTOR
    ra_all[x, y, :, :128] = head_back(grad_qn, query_unit, query_scale, qg).astype(BF16)
    ra_all[x, y, :, 128:] = head_back(grad_kn, key_unit, key_scale, kg).astype(BF16)
    rb_all[x, y, :, :128] = mm_tn(prob_b, grad_attn).astype(BF16)

    own_a, own_b = ra_all.at[x, y], rb_all.at[x, y]
    a_x = [push(own_a, own_a, peer) for peer in x_peers]
    b_y = [push(own_b, own_b, peer) for peer in y_peers]
    b_x = [push(own_b, own_b, peer) for peer in x_peers]
    for o in (1, 2, 3):
        arrive([m_y[o - 1]])
        block = m_all.at[x, lax.rem(y + 4 - o, 4)]
        m_x += [push(block, block, peer) for peer in x_peers]
    arrive(a_x)
    a_y = [push(ra_all.at[:, y], ra_all.at[:, y], peer) for peer in y_peers]
    for o in (1, 2, 3):
        arrive([b_y[o - 1]])
        block = rb_all.at[x, lax.rem(y + 4 - o, 4)]
        b_x += [push(block, block, peer) for peer in x_peers]

    def core_sum(e, r, s):
        own = e[:, pl.ds(c, 1)].reshape(16, 64, FEATURES)
        s[...] = (up(own) + up(r[...])).astype(BF16).reshape(2, 8, 64, FEATURES)

    def scatter_start(s_ref, l_ref, r_ref, s):
        right = lax.rem(z + 5 - s, 8)
        left = lax.rem(z + 3 + s, 8)
        if s == 1:
            first, second = pl.ds(0, 32), pl.ds(32, 32)
            return [
                push(s_ref.at[:, right, first], l_ref.at[0, :, first], z_right),
                push(s_ref.at[:, left, second], r_ref.at[0, :, second], z_left),
            ]
        return [
            push(s_ref.at[:, right], l_ref.at[s - 1], z_right),
            push(s_ref.at[:, left], r_ref.at[s - 1], z_left),
        ]

    def scatter_add(s_ref, l_ref, r_ref, s):
        right = lax.rem(z + 5 - s, 8)
        left = lax.rem(z + 3 + s, 8)
        if s == 2:
            first, second = pl.ds(0, 32), pl.ds(32, 32)
        else:
            first = second = pl.ds(0, 64)
        for at, rows, got in ((right, first, l_ref), (left, second, r_ref)):
            size = 32 if s == 2 else 64
            old = s_ref[:, pl.ds(at, 1), rows].reshape(2, size, FEATURES)
            new = (up(old) + up(got[s - 2, :, rows])).astype(BF16)
            s_ref[:, pl.ds(at, 1), rows] = new.reshape(2, 1, size, FEATURES)

    def scatter_last(s_ref, l_ref, r_ref, f_ref, y_ref, got_ref):
        own = s_ref[:, pl.ds(z, 1)].reshape(2, 64, FEATURES)
        f_ref[...] = up(own) + up(l_ref[3]) + up(r_ref[3])
        y_ref[...] = f_ref[1 - h].astype(BF16)
        return [push(y_ref, got_ref, hi_peer)]

    arrive(m_x)
    for xx in range(4):
        part = mm(m_all[xx].reshape(512, 512), ow[...])
        eo[4 * xx : 4 * xx + 4] = part.astype(BF16).reshape(4, 2, 64, FEATURES)
    ec = [push(eo.at[:, 1 - c], reo, core_peer)]
    arrive(ec)
    core_sum(eo, reo, so)
    ring = scatter_start(so, lo, ro, 1)
    grad_out = mm_tn(m_all[...].reshape(2048, 512), cot_all[...].reshape(2048, FEATURES))
    gwo_ref[...] = grad_out[:128].astype(BF16)
    gwout_ref[...] = grad_out[128:].astype(BF16)
    for s in (2, 3, 4):
        arrive(ring)
        scatter_add(so, lo, ro, s)
        ring = scatter_start(so, lo, ro, s)

    arrive(a_y)
    arrive(b_x)
    for xx in range(4):
        part = mm_nt(ra_all[xx].reshape(512, 256), bw[:, :256])
        part = part + mm_nt(rb_all[xx].reshape(512, 512), bw[:, 256:])
        eg[4 * xx : 4 * xx + 4] = part.astype(BF16).reshape(4, 2, 64, FEATURES)
    ec = [push(eg.at[:, 1 - c], reg, core_peer)]
    arrive(ring)
    yh = scatter_last(so, lo, ro, fo, yo, ryo)
    arrive(ec)
    core_sum(eg, reg, sg)
    ring = scatter_start(sg, lg, rg, 1)
    normed_t = nrm_all[...].reshape(2048, FEATURES)
    part = mm_tn(normed_t, ra_all[...].reshape(2048, 256))
    gwqkv_ref[:, :256] = part.astype(BF16)
    arrive(ring)
    scatter_add(sg, lg, rg, 2)
    ring = scatter_start(sg, lg, rg, 2)
    part = mm_tn(normed_t, rb_all[...].reshape(2048, 512))
    gwqkv_ref[:, 256:] = part[:, :128].astype(BF16)
    gwin_ref[...] = part[:, 128:].astype(BF16)
    for s in (3, 4):
        arrive(ring)
        scatter_add(sg, lg, rg, s)
        ring = scatter_start(sg, lg, rg, s)
    arrive(yh)
    out_ref[...] = (up(x_ref[...]) + fo[h] + up(ryo[...])).astype(BF16)
    arrive(ring)
    yh = scatter_last(sg, lg, rg, fg, yg, ryg)
    arrive(yh)
    local_grad = (fg[h] + up(ryg[...])) * gain_ref[...]
    centred = cen_ref[...]
    stats_b[d] = columns_to_rows(
        jnp.sum(local_grad, 1, keepdims=True),
        jnp.sum(local_grad * centred, 1, keepdims=True),
    )
    arrive([push(stats_b.at[d], stats_b.at[d], peer) for peer in dp_peers])
    sums = jnp.sum(stats_b[...], 0) / D
    first, second = rows_to_columns(sums[0:1], sums[1:2])
    scaling = scl_ref[...][:, 0:1]
    gx_ref[...] = (
        up(cot_ref[...]) + scaling * (local_grad - first - centred * second)
    ).astype(BF16)
    for copy in started:
        copy.wait_send()


def shards(block_input, ln_gain, w_qkv, w_in, w_o, w_out, q_gain, k_gain, cotangent):
    def vmem(*shape):
        return pltpu.VMEM(shape, BF16)

    scratch = [
        vmem(16, 2, 64, 384), vmem(16, 2, 64, 384), vmem(384, 768), vmem(512, 384),
        pltpu.VMEM((16, 8, 128), F32), pltpu.VMEM((16, 8, 128), F32),
        pltpu.VMEM((64, 384), F32), pltpu.VMEM((64, 128), F32),
        vmem(4, 4, 128, 256), vmem(4, 4, 128, 256), vmem(4, 4, 128, 768),
        vmem(3, 4, 128, 256), vmem(3, 4, 128, 256), vmem(3, 4, 128, 768),
        vmem(3, 128, 256), vmem(3, 128, 256), vmem(3, 128, 768),
        vmem(3, 128, 256), vmem(3, 128, 256), vmem(3, 128, 768),
        vmem(4, 4, 128, 512), vmem(4, 4, 128, 256), vmem(4, 4, 128, 512),
        vmem(16, 2, 64, 384), vmem(16, 2, 64, 384), vmem(16, 64, 384), vmem(16, 64, 384),
        vmem(2, 8, 64, 384), vmem(2, 8, 64, 384),
        vmem(4, 2, 64, 384), vmem(4, 2, 64, 384), vmem(4, 2, 64, 384), vmem(4, 2, 64, 384),
        pltpu.VMEM((2, 64, 384), F32), pltpu.VMEM((2, 64, 384), F32),
        vmem(64, 384), vmem(64, 384), vmem(64, 384), vmem(64, 384),
        pltpu.SemaphoreType.DMA((COPIES,)), pltpu.SemaphoreType.DMA((COPIES,)),
    ]
    args = (
        block_input, cotangent, ln_gain.reshape(1, -1), w_qkv, w_in, w_o, w_out, q_gain, k_gain,
    )
    outs = (block_input, cotangent, w_qkv, w_in, w_o, w_out)
    return pl.pallas_call(
        kernel,
        out_shape=tuple(jax.ShapeDtypeStruct(a.shape, BF16) for a in outs),
        in_specs=[pl.BlockSpec(memory_space=pltpu.VMEM)] * len(args),
        out_specs=tuple(pl.BlockSpec(memory_space=pltpu.VMEM) for _ in outs),
        scratch_shapes=scratch,
        compiler_params=pltpu.CompilerParams(
            collective_id=1, has_side_effects=True, vmem_limit_bytes=56 * 2**20
        ),
        name="block",
    )(*args)


def solution(mesh):
    return jax.shard_map(
        shards,
        mesh=mesh,
        in_specs=(
            P("mp", "dp"),
            P("dp"),
            P("dp", "mp"),
            P("dp", "mp"),
            P("mp", "dp"),
            P("mp", "dp"),
            P("mp", None),
            P("mp", None),
            P("mp", "dp"),
        ),
        out_specs=(
            P("mp", "dp"),
            P("mp", "dp"),
            P("dp", "mp"),
            P("dp", "mp"),
            P("mp", "dp"),
            P("mp", "dp"),
        ),
        check_vma=False,
    )
```

```python
import math

import jax
import jax.numpy as jnp
from jax import lax
from jax.experimental import pallas as pl
from jax.experimental.pallas import tpu as pltpu
from jax.sharding import PartitionSpec as P

MESH = pl.DeviceIdType.MESH
D = 6144
FEATURES = 384
N_DP = 16
epsilon = 1e-06
F32 = jnp.float32
BF16 = jnp.bfloat16
FACTOR = 1.0 / math.sqrt(128)
GELU_ROOT = 0.7978845608028654
GELU_CUBE = 0.044715
NT = (((1,), (1,)), ((), ()))
TN = (((0,), (0,)), ((), ()))
COPIES = 300
GATHER_ORDER = (0, 3, 1, 2)
SCATTER_ORDER = (2, 1, 3, 0)


def mm(a, b):
    return jnp.dot(a, b, preferred_element_type=F32)


def mm_nt(a, b):
    return lax.dot_general(a, b, NT, preferred_element_type=F32)


def mm_tn(a, b):
    return lax.dot_general(a, b, TN, preferred_element_type=F32)


def up(v):
    return v.astype(F32)


def head_norm(values, gain):
    centre = values - jnp.mean(values, -1, keepdims=True)
    scaling = 1.0 / jnp.sqrt(jnp.mean(centre * centre, -1, keepdims=True) + epsilon)
    unit = centre * scaling
    return (unit * gain, unit, scaling)


def head_back(grad, unit, scaling, gain):
    local_grad = grad * gain
    return scaling * (
        local_grad
        - jnp.mean(local_grad, -1, keepdims=True)
        - unit * jnp.mean(local_grad * unit, -1, keepdims=True)
    )


def columns_to_rows(first, second):
    lane = lax.broadcasted_iota(jnp.int32, (64, 128), 1)
    block = jnp.where(lane == 0, first, jnp.where(lane == 1, second, 0.0))
    block = jnp.concatenate([block, jnp.zeros((64, 128), F32)], 0)
    return block.T[:8]


def rows_to_columns(first, second):
    row = lax.broadcasted_iota(jnp.int32, (128, 128), 0)
    block = jnp.where(row == 0, first, jnp.where(row == 1, second, 0.0)).T
    return block[:64, 0:1], block[:64, 1:2]


def kernel(
    x_ref, cot_ref, gain_ref, wqkv_ref, win_ref, wo_ref, wout_ref, qg_ref, kg_ref,
    out_ref, gx_ref, gwqkv_ref, gwin_ref, gwo_ref, gwout_ref,
    cot_all, nrm_all, bw, ow, stats, stats_b, cen_ref, scl_ref,
    g1, rg1, s1, tg1,
    g2, hl2, hr2, fl2, fr2, s2, t2,
    fp, hlf, hrf, flf, frf, sf, tf,
    m_all, ra_all, rb_all, eo, eg, reo, reg, so, sg, lo, ro, lg, rg, fo, fg, yo, yg, ryo, ryg,
    send, recv,
):
    d = lax.axis_index("dp")
    m = lax.axis_index("mp")
    x, y = d // 4, lax.rem(d, 4)
    h, z, c = m // 16, lax.rem(m // 2, 8), lax.rem(m, 2)

    def dp_at(xx, yy):
        return (xx * 4 + yy, m)

    def around(v, o):
        return lax.rem(v + o, 4)

    x_peers = [dp_at(around(x, o), y) for o in (1, 2, 3)]
    y_peers = [dp_at(x, around(y, o)) for o in (1, 2, 3)]
    x_right, x_left = x_peers[0], x_peers[2]
    hi_peer = (d, (1 - h) * 16 + z * 2 + c)
    z_right = (d, h * 16 + lax.rem(z + 1, 8) * 2 + c)
    z_left = (d, h * 16 + lax.rem(z + 7, 8) * 2 + c)
    core_peer = (d, m + 1 - 2 * c)

    barrier = pltpu.get_barrier_semaphore()
    everyone = x_peers + y_peers + [hi_peer, z_right, z_left, core_peer]
    for peer in everyone:
        pl.semaphore_signal(barrier, inc=1, device_id=peer, device_id_type=MESH)

    started = []
    slots = []

    def take(n):
        first = len(slots)
        slots.extend([None] * n)
        return first

    def push(src, dst, peer, when=None, at=None):
        n = len(started)
        copy = pltpu.make_async_remote_copy(
            src_ref=src, dst_ref=dst, send_sem=send.at[n],
            recv_sem=recv.at[take(1) if at is None else at],
            device_id=peer, device_id_type=MESH,
        )
        started.append((copy, when))
        if when is None:
            copy.start()
        else:
            pl.when(when)(copy.start)
        return copy

    def arrive(copies):
        for copy in copies:
            copy.wait_recv()

    def expect(dst, at):
        pltpu.make_async_remote_copy(
            src_ref=dst, dst_ref=dst, send_sem=send.at[0], recv_sem=recv.at[at],
            device_id=core_peer, device_id_type=MESH,
        ).wait_recv()

    gain = gain_ref[...][None, :]
    cot_all[z, h, c] = cot_ref[...]
    inputs = up(x_ref[...])
    local_mean = jnp.sum(inputs, 1, keepdims=True) / FEATURES
    local_centre = inputs - local_mean
    local_m2 = jnp.sum(local_centre * local_centre, 1, keepdims=True)
    stats[x, y] = columns_to_rows(local_mean, local_m2)
    bw[:, :384] = wqkv_ref[...]
    bw[:, 384:] = win_ref[...]
    ow[:128] = wo_ref[...]
    ow[128:] = wout_ref[...]
    pl.semaphore_wait(barrier, len(everyone))

    def hi_start(a):
        return [push(a.at[z, h, c], a.at[z, h, c], hi_peer)]

    def ring_start(a, kind, s):
        hh = h if kind == 0 else 1 - h
        right = lax.rem(z + 9 - s, 8)
        left = lax.rem(z + s - 1, 8)
        if s == 4:
            first, second = pl.ds(0, 32), pl.ds(32, 32)
            return [
                push(a.at[right, hh, c, first], a.at[right, hh, c, first], z_right),
                push(a.at[left, hh, c, second], a.at[left, hh, c, second], z_left),
            ]
        return [
            push(a.at[right, hh, c], a.at[right, hh, c], z_right),
            push(a.at[left, hh, c], a.at[left, hh, c], z_left),
        ]

    def core_start(a, s):
        ats = [z] if s == 0 else [lax.rem(z + s, 8)]
        if s in (1, 2, 3):
            ats.append(lax.rem(z + 8 - s, 8))
        return [push(a.at[at, :, c], a.at[at, :, c], core_peer) for at in ats]

    class Gather:
        def __init__(self, a):
            self.a = a
            self.hi = hi_start(a)
            self.own = ring_start(a, 0, 1)
            self.other = None
            self.core = {}

        def first_other(self):
            arrive(self.hi)
            self.other = ring_start(self.a, 1, 1)
            self.core[0] = core_start(self.a, 0)

        def own_step(self, s):
            arrive(self.own)
            self.own = ring_start(self.a, 0, s) if s < 5 else []

        def other_step(self, s):
            arrive(self.other)
            self.other = ring_start(self.a, 1, s) if s < 5 else []
            self.core[s - 1] = core_start(self.a, s - 1)

        def ready(self, s):
            arrive(self.core.pop(s))

    def rows_of(a, yy):
        parts = []
        for xx in range(4):
            at = lax.rem(z + 2 * yy + xx % 2, 8)
            parts.append(a[at, xx // 2].reshape(128, FEATURES))
        return jnp.concatenate(parts, 0)

    class Scatter:
        def __init__(self, part, hl, hr, fl, fr, s, t):
            self.part, self.hl, self.hr, self.fl, self.fr = part, hl, hr, fl, fr
            self.s, self.t = s, t
            self.base = take(4)
            self.half, self.full = {}, {}

        def send_half(self, yy):
            far = around(x, 2)
            first, second = pl.ds(0, 64), pl.ds(64, 64)
            self.half[yy] = [
                push(self.part.at[far, yy, first], self.hl.at[yy], x_right),
                push(self.part.at[far, yy, second], self.hr.at[yy], x_left),
            ]

        def send_full(self, yy):
            arrive(self.half.pop(yy))
            right, left = around(x, 1), around(x, 3)
            new = up(self.part[right, yy, :64]) + up(self.hl[yy])
            self.part[right, yy, :64] = new.astype(BF16)
            a = push(self.part.at[right, yy], self.fl.at[yy], x_right)
            new = up(self.part[left, yy, 64:]) + up(self.hr[yy])
            self.part[left, yy, 64:] = new.astype(BF16)
            b = push(self.part.at[left, yy], self.fr.at[yy], x_left)
            self.full[yy] = [a, b]

        def send_y(self, yy):
            arrive(self.full.pop(yy))
            total = up(self.part[x, yy]) + up(self.fl[yy]) + up(self.fr[yy])
            self.s[yy] = total.astype(BF16)
            o = lax.rem(yy - y + 4, 4)
            slot = lax.rem(o + 3, 4)
            push(
                self.s.at[yy], self.t.at[slot], dp_at(x, yy), when=o != 0, at=self.base + slot
            )

        def result(self):
            total = up(self.part[x, y]) + up(self.fl[y]) + up(self.fr[y])
            for i in range(3):
                expect(self.t.at[i], self.base + i)
                total = total + up(self.t[i])
            return total

    def sums_x(ref):
        return [push(ref.at[x, y], ref.at[x, y], peer) for peer in x_peers]

    def sums_y(ref):
        return [push(ref.at[:, y], ref.at[:, y], peer) for peer in y_peers]

    st = sums_x(stats)
    cg = Gather(cot_all)
    arrive(st)
    st = sums_y(stats)
    cg.first_other()
    cg.own_step(2)
    arrive(st)
    every = stats[...].reshape(16, 8, 128)
    mean_row = jnp.sum(every[:, 0:1, :], 0) / N_DP
    apart = every[:, 0:1, :] - mean_row[None]
    m2_row = jnp.sum(every[:, 1:2, :], 0) + FEATURES * jnp.sum(apart * apart, 0)
    scaling_row = 1.0 / jnp.sqrt(m2_row / D + epsilon)
    mean, scaling = rows_to_columns(mean_row, scaling_row)
    centred = (inputs - mean) * scaling
    nrm_all[z, h, c] = (centred * gain).astype(BF16)
    ng = Gather(nrm_all)
    cen_ref[...] = centred
    scl_ref[...] = jnp.broadcast_to(scaling, (64, 128))

    gs = Scatter(g2, hl2, hr2, fl2, fr2, s2, t2)
    fs = Scatter(fp, hlf, hrf, flf, frf, sf, tf)
    q_base = take(4)

    def g_product(yy):
        product = mm_nt(rows_of(cot_all, yy), ow[...]).astype(BF16)
        g2[:, yy] = product[:, 128:].reshape(4, 128, 384)
        gs.send_half(yy)
        g1[:, yy] = product[:, :128].reshape(4, 128, 128)
        o = lax.rem(yy - y + 4, 4)
        slot = lax.rem(o + 3, 4)
        push(g1.at[:, yy], rg1.at[slot], dp_at(x, yy), when=o != 0, at=q_base + slot)

    def f_product(yy):
        product = mm(rows_of(nrm_all, yy), bw[...]).astype(BF16)
        fp[:, yy] = product.reshape(4, 128, 768)
        fs.send_half(yy)

    cg.other_step(2)
    cg.own_step(3)
    ng.first_other()
    ng.own_step(2)
    cg.other_step(3)
    cg.own_step(4)
    cg.ready(0)
    cg.ready(1)
    g_product(0)
    ng.other_step(2)
    ng.own_step(3)
    cg.other_step(4)
    cg.own_step(5)
    cg.ready(2)
    g_product(3)
    gs.send_full(0)
    ng.other_step(3)
    ng.own_step(4)
    cg.other_step(5)
    cg.ready(3)
    g_product(1)
    gs.send_full(3)
    ng.ready(0)
    ng.ready(1)
    f_product(0)
    gs.send_y(0)
    ng.other_step(4)
    ng.own_step(5)
    cg.ready(4)
    g_product(2)
    gs.send_full(1)
    ng.ready(2)
    f_product(3)
    fs.send_full(0)
    gs.send_y(3)
    ng.other_step(5)
    gs.send_full(2)
    ng.ready(3)
    f_product(1)
    fs.send_full(3)
    gs.send_y(1)
    fs.send_y(0)
    ng.ready(4)
    f_product(2)
    fs.send_full(1)
    gs.send_y(2)
    fs.send_y(3)
    fs.send_full(2)
    total = up(g1[:, y])
    for i in range(3):
        expect(rg1.at[i], q_base + i)
        total = total + up(rg1[i])
    s1[...] = total.astype(BF16)
    tq = [push(s1.at[around(x, o)], tg1.at[o - 1], x_peers[o - 1]) for o in (1, 2, 3)]
    fs.send_y(1)
    grad_act = gs.result()
    arrive(tq)
    grad_attn = up(g1[x, y]) + up(tg1[0]) + up(tg1[1]) + up(tg1[2])
    for i in range(3):
        grad_attn = grad_attn + up(rg1[i, x])
    fs.send_y(2)
    features = fs.result()

    qg, kg = qg_ref[...], kg_ref[...]
    queries, query_unit, query_scale = head_norm(features[:, :128], qg)
    keys, key_unit, key_scale = head_norm(features[:, 128:256], kg)
    query_b, key_b = queries.astype(BF16), keys.astype(BF16)
    value_b = features[:, 256:384].astype(BF16)
    pre = features[:, 384:]
    expo = jnp.exp(mm_nt(query_b, key_b) * FACTOR)
    prob = expo / jnp.sum(expo, -1, keepdims=True)
    prob_b = prob.astype(BF16)
    inner = GELU_ROOT * (pre + GELU_CUBE * (pre * pre * pre))
    bend = jnp.tanh(inner)
    m_all[x, y, :, :128] = mm(prob_b, value_b).astype(BF16)
    m_all[x, y, :, 128:] = (0.5 * pre * (1.0 + bend)).astype(BF16)
    own_m = m_all.at[x, y]
    m_y = [push(own_m, own_m, peer) for peer in y_peers]

    class Spread:
        def __init__(self, a):
            self.a, self.near, self.far = a, {}, {}

        def send_near(self, k, yy):
            block = self.a.at[x, yy]
            self.near[k] = [push(block, block, x_right), push(block, block, x_left)]

        def send_far(self, k, yy):
            arrive(self.near.pop(k))
            first = self.a.at[around(x, 3), yy, pl.ds(0, 64)]
            second = self.a.at[around(x, 1), yy, pl.ds(64, 64)]
            self.far[k] = [push(first, first, x_right), push(second, second, x_left)]

        def ready(self, k):
            arrive(self.far.pop(k))

    ms = Spread(m_all)
    ms.send_near(0, y)
    slope = 0.5 * (1.0 + bend) + 0.5 * pre * (1.0 - bend * bend) * (
        GELU_ROOT * (1.0 + 3.0 * GELU_CUBE * (pre * pre))
    )
    grad_attn = grad_attn.astype(BF16)
    rb_all[x, y, :, 256:] = (grad_act * slope).astype(BF16)
    dprob = mm_nt(grad_attn, value_b)
    delta = jnp.sum(prob * dprob, -1, keepdims=True)
    dscore = (prob * (dprob - delta)).astype(BF16)
    grad_qn = mm(dscore, key_b) * FACTOR
    grad_kn = mm_tn(dscore, query_b) * FACTOR
    ra_all[x, y] = head_back(grad_qn, query_unit, query_scale, qg).astype(BF16)
    rb_all[x, y, :, :128] = head_back(grad_kn, key_unit, key_scale, kg).astype(BF16)
    rb_all[x, y, :, 128:256] = mm_tn(prob_b, grad_attn).astype(BF16)
    own_a, own_b = ra_all.at[x, y], rb_all.at[x, y]
    a_x = [push(own_a, own_a, peer) for peer in x_peers]
    b_base = take(4)
    for o in (1, 2, 3):
        push(own_b, own_b, y_peers[o - 1], at=b_base + o - 1)
    rs = Spread(rb_all)

    def r_near(yy):
        o = lax.rem(y - yy + 4, 4)

        @pl.when(o != 0)
        def _():
            expect(rb_all.at[x, yy], b_base + lax.rem(o + 3, 4))

        rs.send_near(yy, yy)

    for o in (1, 2, 3):
        arrive([m_y[o - 1]])
        ms.send_near(o, around(y, 4 - o))
        ms.send_far(o - 1, around(y, 5 - o))
    arrive(a_x)
    a_y = [push(ra_all.at[:, y], ra_all.at[:, y], peer) for peer in y_peers]
    r_near(2)
    ms.send_far(3, around(y, 1))
    r_near(1)
    for k in range(4):
        ms.ready(k)

    class Reduce:
        def __init__(self, e, r, s, left, right, f, yv, got):
            self.e, self.r, self.s, self.left, self.right = e, r, s, left, right
            self.f, self.yv, self.got = f, yv, got
            self.core, self.ring = {}, None

        def chunk(self, yy, part):
            self.e[yy] = part.astype(BF16).reshape(4, 2, 64, FEATURES)
            self.core[yy] = [push(self.e.at[yy, :, 1 - c], self.r.at[yy], core_peer)]

        def core_sum(self, yy):
            arrive(self.core.pop(yy))
            own = self.e[yy, :, pl.ds(c, 1)].reshape(4, 64, FEATURES)
            total = (up(own) + up(self.r[yy])).astype(BF16)
            for xx in range(4):
                self.s[2 * yy + xx % 2, xx // 2] = total[xx]

        def step(self, s):
            if s == 1:
                first, second = pl.ds(0, 32), pl.ds(32, 32)
                self.ring = [
                    push(self.s.at[4, :, first], self.left.at[0, :, first], z_right),
                    push(self.s.at[4, :, second], self.right.at[0, :, second], z_left),
                ]
                return
            first, second = (slice(0, 32), slice(32, 64)) if s == 2 else (slice(None),) * 2
            a, b = self.ring
            arrive([a])
            new = up(self.s[5 - s, :, first]) + up(self.left[s - 2, :, first])
            self.s[5 - s, :, first] = new.astype(BF16)
            a = push(self.s.at[5 - s], self.left.at[s - 1], z_right)
            arrive([b])
            new = up(self.s[3 + s, :, second]) + up(self.right[s - 2, :, second])
            self.s[3 + s, :, second] = new.astype(BF16)
            b = push(self.s.at[3 + s], self.right.at[s - 1], z_left)
            self.ring = [a, b]

        def last(self):
            arrive(self.ring)
            self.f[...] = up(self.s[0]) + up(self.left[3]) + up(self.right[3])
            self.yv[...] = self.f[1 - h].astype(BF16)
            self.hi = [push(self.yv, self.got, hi_peer)]

        def result(self):
            arrive(self.hi)
            return self.f[h] + up(self.got[...])

    outs = Reduce(eo, reo, so, lo, ro, fo, yo, ryo)
    grads = Reduce(eg, reg, sg, lg, rg, fg, yg, ryg)

    def grad_product(yy):
        rs.ready(yy)
        part = mm_nt(ra_all[:, yy].reshape(512, 128), bw[:, :128])
        part = part + mm_nt(rb_all[:, yy].reshape(512, 640), bw[:, 128:])
        grads.chunk(yy, part)

    for yy in SCATTER_ORDER:
        outs.chunk(yy, mm(m_all[:, yy].reshape(512, 512), ow[...]))
    rs.send_far(2, 2)
    r_near(3)
    for yy in SCATTER_ORDER:
        outs.core_sum(yy)
    outs.step(1)
    rs.send_far(1, 1)
    r_near(0)
    weight = jnp.zeros((512, FEATURES), F32)
    for yy in range(4):
        weight = weight + mm_tn(m_all[:, yy].reshape(512, 512), rows_of(cot_all, yy))
    gwo_ref[...] = weight[:128].astype(BF16)
    gwout_ref[...] = weight[128:].astype(BF16)
    outs.step(2)
    arrive(a_y)
    grad_product(2)
    rs.send_far(3, 3)
    outs.step(3)
    grad_product(1)
    grads.core_sum(2)
    grads.step(1)
    rs.send_far(0, 0)
    outs.step(4)
    grad_product(3)
    grads.core_sum(1)
    grads.step(2)
    outs.last()
    grad_product(0)
    grads.core_sum(3)
    grads.step(3)
    normed_rows = [rows_of(nrm_all, yy) for yy in range(4)]
    weight = jnp.zeros((FEATURES, 128), F32)
    for yy in range(4):
        weight = weight + mm_tn(normed_rows[yy], ra_all[:, yy].reshape(512, 128))
    gwqkv_ref[:, :128] = weight.astype(BF16)
    out_ref[...] = (up(x_ref[...]) + outs.result()).astype(BF16)
    grads.core_sum(0)
    grads.step(4)
    weight = jnp.zeros((FEATURES, 640), F32)
    for yy in range(4):
        weight = weight + mm_tn(normed_rows[yy], rb_all[:, yy].reshape(512, 640))
    gwqkv_ref[:, 128:] = weight[:, :256].astype(BF16)
    gwin_ref[...] = weight[:, 256:].astype(BF16)
    grads.last()
    local_grad = grads.result() * gain
    centred = cen_ref[...]
    stats_b[x, y] = columns_to_rows(
        jnp.sum(local_grad, 1, keepdims=True),
        jnp.sum(local_grad * centred, 1, keepdims=True),
    )
    arrive(sums_x(stats_b))
    arrive(sums_y(stats_b))
    sums = jnp.sum(stats_b[...].reshape(16, 8, 128), 0) / D
    first, second = rows_to_columns(sums[0:1], sums[1:2])
    scaling = scl_ref[...][:, 0:1]
    gx_ref[...] = (
        up(cot_ref[...]) + scaling * (local_grad - first - centred * second)
    ).astype(BF16)
    for copy, when in started:
        if when is None:
            copy.wait_send()
        else:
            pl.when(when)(copy.wait_send)


def place(*refs):
    n = len(refs) // 2
    for i in range(n):
        refs[n + i][...] = refs[i][...]


def shards(block_input, ln_gain, w_qkv, w_in, w_o, w_out, q_gain, k_gain, cotangent):
    def vmem(*shape):
        return pltpu.VMEM(shape, BF16)

    def scatter(cols):
        return [
            vmem(4, 4, 128, cols), vmem(4, 64, cols), vmem(4, 64, cols),
            vmem(4, 128, cols), vmem(4, 128, cols), vmem(4, 128, cols), vmem(4, 128, cols),
        ]

    ring = vmem(4, 2, 64, 384)
    scratch = [
        vmem(8, 2, 2, 64, 384), vmem(8, 2, 2, 64, 384), vmem(384, 768), vmem(512, 384),
        pltpu.VMEM((4, 4, 8, 128), F32), pltpu.VMEM((4, 4, 8, 128), F32),
        pltpu.VMEM((64, 384), F32), pltpu.VMEM((64, 128), F32),
        vmem(4, 4, 128, 128), vmem(4, 4, 128, 128), vmem(4, 128, 128), vmem(3, 128, 128),
        *scatter(384), *scatter(768),
        vmem(4, 4, 128, 512), vmem(4, 4, 128, 128), vmem(4, 4, 128, 640),
        vmem(4, 4, 2, 64, 384), vmem(4, 4, 2, 64, 384), vmem(4, 4, 64, 384), vmem(4, 4, 64, 384),
        vmem(8, 2, 64, 384), vmem(8, 2, 64, 384), ring, ring, ring, ring,
        pltpu.VMEM((2, 64, 384), F32), pltpu.VMEM((2, 64, 384), F32),
        vmem(64, 384), vmem(64, 384), vmem(64, 384), vmem(64, 384),
        pltpu.SemaphoreType.DMA((COPIES,)), pltpu.SemaphoreType.DMA((COPIES,)),
    ]
    args = (block_input, cotangent, ln_gain, w_qkv, w_in, w_o, w_out, q_gain, k_gain)
    outs = (block_input, cotangent, w_qkv, w_in, w_o, w_out)
    shapes = tuple(jax.ShapeDtypeStruct(a.shape, BF16) for a in outs)
    results = pl.pallas_call(
        kernel,
        out_shape=shapes,
        in_specs=[pl.BlockSpec(memory_space=pltpu.VMEM)] * len(args),
        out_specs=tuple(pl.BlockSpec(memory_space=pltpu.VMEM) for _ in outs),
        scratch_shapes=scratch,
        compiler_params=pltpu.CompilerParams(
            collective_id=1, has_side_effects=True, vmem_limit_bytes=56 * 2**20
        ),
        name="block",
    )(*args)
    return pl.pallas_call(
        place,
        out_shape=shapes,
        in_specs=[pl.BlockSpec(memory_space=pltpu.VMEM)] * len(outs),
        out_specs=tuple(pl.BlockSpec(memory_space=pltpu.VMEM) for _ in outs),
        name="place",
    )(*results)


def solution(mesh):
    return jax.shard_map(
        shards,
        mesh=mesh,
        in_specs=(
            P("mp", "dp"),
            P("dp"),
            P("dp", "mp"),
            P("dp", "mp"),
            P("mp", "dp"),
            P("mp", "dp"),
            P("mp", None),
            P("mp", None),
            P("mp", "dp"),
        ),
        out_specs=(
            P("mp", "dp"),
            P("mp", "dp"),
            P("dp", "mp"),
            P("dp", "mp"),
            P("mp", "dp"),
            P("mp", "dp"),
        ),
        check_vma=False,
    )
```

```python
import math

import jax
import jax.numpy as jnp
from jax import lax
from jax.experimental import pallas as pl
from jax.experimental.pallas import tpu as pltpu
from jax.sharding import PartitionSpec as P

MESH = pl.DeviceIdType.MESH
D = 6144
FEATURES = 384
N_DP = 16
epsilon = 1e-06
F32 = jnp.float32
BF16 = jnp.bfloat16
FACTOR = 1.0 / math.sqrt(128)
GELU_ROOT = 0.7978845608028654
GELU_CUBE = 0.044715
NT = (((1,), (1,)), ((), ()))
TN = (((0,), (0,)), ((), ()))
SENDS = 64
ARRIVALS = 188
SCATTER_ORDER = (2, 1, 3, 0)


def mm(a, b):
    return jnp.dot(a, b, preferred_element_type=F32)


def mm_nt(a, b):
    return lax.dot_general(a, b, NT, preferred_element_type=F32)


def mm_tn(a, b):
    return lax.dot_general(a, b, TN, preferred_element_type=F32)


def up(v):
    return v.astype(F32)


def head_norm(values, gain):
    centre = values - jnp.mean(values, -1, keepdims=True)
    scaling = 1.0 / jnp.sqrt(jnp.mean(centre * centre, -1, keepdims=True) + epsilon)
    unit = centre * scaling
    return (unit * gain, unit, scaling)


def head_back(grad, unit, scaling, gain):
    local_grad = grad * gain
    return scaling * (
        local_grad
        - jnp.mean(local_grad, -1, keepdims=True)
        - unit * jnp.mean(local_grad * unit, -1, keepdims=True)
    )


def columns_to_rows(first, second):
    lane = lax.broadcasted_iota(jnp.int32, (64, 128), 1)
    block = jnp.where(lane == 0, first, jnp.where(lane == 1, second, 0.0))
    block = jnp.concatenate([block, jnp.zeros((64, 128), F32)], 0)
    return block.T[:8]


def rows_to_columns(first, second):
    row = lax.broadcasted_iota(jnp.int32, (128, 128), 0)
    block = jnp.where(row == 0, first, jnp.where(row == 1, second, 0.0)).T
    return block[:64, 0:1], block[:64, 1:2]


def kernel(
    x_ref, cot_ref, gain_ref, wqkv_ref, win_ref, wo_ref, wout_ref, qg_ref, kg_ref,
    out_ref, gx_ref, gwqkv_ref, gwin_ref, gwo_ref, gwout_ref,
    cot_all, nrm_all, bw, ow, stats, stats_b, cen_ref, scl_ref,
    g2, hl2, hr2, fl2, fr2, s2, t2,
    fp, hlf, hrf, flf, frf, sf, tf,
    ep, hle, hre, fle, fre, se, te,
    m_all, r_all, eo, eg, reo, reg, so, sg, lo, ro, lg, rg, fo, fg, yo, yg, ryo, ryg,
    send, recv,
):
    d = lax.axis_index("dp")
    m = lax.axis_index("mp")
    x, y = d // 4, lax.rem(d, 4)
    h, z, c = m // 16, lax.rem(m // 2, 8), lax.rem(m, 2)

    def dp_at(xx, yy):
        return (xx * 4 + yy, m)

    def around(v, o):
        return lax.rem(v + o, 4)

    x_peers = [dp_at(around(x, o), y) for o in (1, 2, 3)]
    y_peers = [dp_at(x, around(y, o)) for o in (1, 2, 3)]
    x_right, x_left = x_peers[0], x_peers[2]
    hi_peer = (d, (1 - h) * 16 + z * 2 + c)
    z_right = (d, h * 16 + lax.rem(z + 1, 8) * 2 + c)
    z_left = (d, h * 16 + lax.rem(z + 7, 8) * 2 + c)
    core_peer = (d, m + 1 - 2 * c)

    barrier = pltpu.get_barrier_semaphore()
    everyone = x_peers + y_peers + [hi_peer, z_right, z_left, core_peer]
    for peer in everyone:
        pl.semaphore_signal(barrier, inc=1, device_id=peer, device_id_type=MESH)

    started = []
    slots = []

    def take(n):
        first = len(slots)
        slots.extend([None] * n)
        return first

    def finish(copy, when):
        if when is None:
            copy.wait_send()
        else:
            pl.when(when)(copy.wait_send)

    def push(src, dst, peer, when=None, at=None):
        n = len(started)
        if n >= SENDS:
            finish(*started[n - SENDS])
        copy = pltpu.make_async_remote_copy(
            src_ref=src, dst_ref=dst, send_sem=send.at[n % SENDS],
            recv_sem=recv.at[take(1) if at is None else at],
            device_id=peer, device_id_type=MESH,
        )
        started.append((copy, when))
        if when is None:
            copy.start()
        else:
            pl.when(when)(copy.start)
        return copy

    def arrive(copies):
        for copy in copies:
            copy.wait_recv()

    def expect(dst, at):
        pltpu.make_async_remote_copy(
            src_ref=dst, dst_ref=dst, send_sem=send.at[0], recv_sem=recv.at[at],
            device_id=core_peer, device_id_type=MESH,
        ).wait_recv()

    gain = gain_ref[...][None, :]
    cot_all[z, h, c] = cot_ref[...]
    inputs = up(x_ref[...])
    local_mean = jnp.sum(inputs, 1, keepdims=True) / FEATURES
    local_centre = inputs - local_mean
    local_m2 = jnp.sum(local_centre * local_centre, 1, keepdims=True)
    stats[x, y] = columns_to_rows(local_mean, local_m2)
    bw[:, :384] = wqkv_ref[...]
    bw[:, 384:] = win_ref[...]
    ow[:128] = wo_ref[...]
    ow[128:] = wout_ref[...]
    pl.semaphore_wait(barrier, len(everyone))

    def hi_start(a):
        return [push(a.at[z, h, c], a.at[z, h, c], hi_peer)]

    def ring_start(a, kind, s):
        hh = h if kind == 0 else 1 - h
        right = lax.rem(z + 9 - s, 8)
        left = lax.rem(z + s - 1, 8)
        if s == 4:
            first, second = pl.ds(0, 32), pl.ds(32, 32)
            return [
                push(a.at[right, hh, c, first], a.at[right, hh, c, first], z_right),
                push(a.at[left, hh, c, second], a.at[left, hh, c, second], z_left),
            ]
        return [
            push(a.at[right, hh, c], a.at[right, hh, c], z_right),
            push(a.at[left, hh, c], a.at[left, hh, c], z_left),
        ]

    def core_start(a, s):
        ats = [z] if s == 0 else [lax.rem(z + s, 8)]
        if s in (1, 2, 3):
            ats.append(lax.rem(z + 8 - s, 8))
        return [push(a.at[at, :, c], a.at[at, :, c], core_peer) for at in ats]

    class Gather:
        def __init__(self, a):
            self.a = a
            self.hi = hi_start(a)
            self.own = ring_start(a, 0, 1)
            self.other = None
            self.core = {}

        def first_other(self):
            arrive(self.hi)
            self.other = ring_start(self.a, 1, 1)
            self.core[0] = core_start(self.a, 0)

        def own_step(self, s):
            arrive(self.own)
            self.own = ring_start(self.a, 0, s) if s < 5 else []

        def other_step(self, s):
            arrive(self.other)
            self.other = ring_start(self.a, 1, s) if s < 5 else []
            self.core[s - 1] = core_start(self.a, s - 1)

        def ready(self, s):
            arrive(self.core.pop(s))

    def rows_of(a, yy):
        parts = []
        for xx in range(4):
            at = lax.rem(z + 2 * yy + xx % 2, 8)
            parts.append(a[at, xx // 2].reshape(128, FEATURES))
        return jnp.concatenate(parts, 0)

    class Scatter:
        def __init__(self, part, hl, hr, fl, fr, s, t):
            self.part, self.hl, self.hr, self.fl, self.fr = part, hl, hr, fl, fr
            self.s, self.t = s, t
            self.base = take(4)
            self.half, self.full = {}, {}

        def send_half(self, yy):
            far = around(x, 2)
            first, second = pl.ds(0, 64), pl.ds(64, 64)
            self.half[yy] = [
                push(self.part.at[far, yy, first], self.hl.at[yy], x_right),
                push(self.part.at[far, yy, second], self.hr.at[yy], x_left),
            ]

        def send_full(self, yy):
            arrive(self.half.pop(yy))
            right, left = around(x, 1), around(x, 3)
            new = up(self.part[right, yy, :64]) + up(self.hl[yy])
            self.part[right, yy, :64] = new.astype(BF16)
            a = push(self.part.at[right, yy], self.fl.at[yy], x_right)
            new = up(self.part[left, yy, 64:]) + up(self.hr[yy])
            self.part[left, yy, 64:] = new.astype(BF16)
            b = push(self.part.at[left, yy], self.fr.at[yy], x_left)
            self.full[yy] = [a, b]

        def send_y(self, yy):
            arrive(self.full.pop(yy))
            total = up(self.part[x, yy]) + up(self.fl[yy]) + up(self.fr[yy])
            self.s[yy] = total.astype(BF16)
            o = lax.rem(yy - y + 4, 4)
            slot = lax.rem(o + 3, 4)
            push(
                self.s.at[yy], self.t.at[slot], dp_at(x, yy), when=o != 0, at=self.base + slot
            )

        def result(self):
            total = up(self.part[x, y]) + up(self.fl[y]) + up(self.fr[y])
            for i in range(3):
                expect(self.t.at[i], self.base + i)
                total = total + up(self.t[i])
            return total

    def sums_x(ref):
        return [push(ref.at[x, y], ref.at[x, y], peer) for peer in x_peers]

    def sums_y(ref):
        return [push(ref.at[:, y], ref.at[:, y], peer) for peer in y_peers]

    st = sums_x(stats)
    cg = Gather(cot_all)
    arrive(st)
    st = sums_y(stats)
    cg.first_other()
    cg.own_step(2)
    arrive(st)
    every = stats[...].reshape(16, 8, 128)
    mean_row = jnp.sum(every[:, 0:1, :], 0) / N_DP
    apart = every[:, 0:1, :] - mean_row[None]
    m2_row = jnp.sum(every[:, 1:2, :], 0) + FEATURES * jnp.sum(apart * apart, 0)
    scaling_row = 1.0 / jnp.sqrt(m2_row / D + epsilon)
    mean, scaling = rows_to_columns(mean_row, scaling_row)
    centred = (inputs - mean) * scaling
    nrm_all[z, h, c] = (centred * gain).astype(BF16)
    ng = Gather(nrm_all)
    cen_ref[...] = centred
    scl_ref[...] = jnp.broadcast_to(scaling, (64, 128))

    gs = Scatter(g2, hl2, hr2, fl2, fr2, s2, t2)
    fs = Scatter(fp, hlf, hrf, flf, frf, sf, tf)
    es = Scatter(ep, hle, hre, fle, fre, se, te)

    def g_product(yy):
        product = mm_nt(rows_of(cot_all, yy), ow[...]).astype(BF16)
        g2[:, yy] = product.reshape(4, 128, 512)
        gs.send_half(yy)

    def f_product(yy):
        product = mm(rows_of(nrm_all, yy), bw[...]).astype(BF16)
        fp[:, yy] = product[:, :384].reshape(4, 128, 384)
        fs.send_half(yy)
        ep[:, yy] = product[:, 384:].reshape(4, 128, 384)
        es.send_half(yy)

    cg.other_step(2)
    cg.own_step(3)
    ng.first_other()
    ng.own_step(2)
    cg.other_step(3)
    cg.own_step(4)
    cg.ready(0)
    cg.ready(1)
    g_product(0)
    ng.other_step(2)
    ng.own_step(3)
    cg.other_step(4)
    cg.own_step(5)
    cg.ready(2)
    g_product(3)
    gs.send_full(0)
    ng.other_step(3)
    ng.own_step(4)
    cg.other_step(5)
    ng.ready(0)
    ng.ready(1)
    f_product(0)
    gs.send_full(3)
    gs.send_y(0)
    ng.other_step(4)
    ng.own_step(5)
    ng.ready(2)
    f_product(3)
    fs.send_full(0)
    es.send_full(0)
    ng.other_step(5)
    gs.send_y(3)
    ng.ready(3)
    f_product(1)
    fs.send_full(3)
    es.send_full(3)
    fs.send_y(0)
    ng.ready(4)
    f_product(2)
    es.send_y(0)
    fs.send_full(1)
    es.send_full(1)
    fs.send_y(3)
    cg.ready(3)
    cg.ready(4)
    g_product(1)
    fs.send_full(2)
    es.send_full(2)
    es.send_y(3)
    g_product(2)
    fs.send_y(1)
    es.send_y(1)
    gs.send_full(1)
    fs.send_y(2)
    es.send_y(2)
    gs.send_full(2)
    gs.send_y(1)
    qkv = fs.result()

    qg, kg = qg_ref[...], kg_ref[...]
    queries, query_unit, query_scale = head_norm(qkv[:, :128], qg)
    keys, key_unit, key_scale = head_norm(qkv[:, 128:256], kg)
    query_b, key_b = queries.astype(BF16), keys.astype(BF16)
    value_b = qkv[:, 256:].astype(BF16)
    expo = jnp.exp(mm_nt(query_b, key_b) * FACTOR)
    prob = expo / jnp.sum(expo, -1, keepdims=True)
    prob_b = prob.astype(BF16)
    m_all[x, y, :, :128] = mm(prob_b, value_b).astype(BF16)
    pre = es.result()
    inner = GELU_ROOT * (pre + GELU_CUBE * (pre * pre * pre))
    bend = jnp.tanh(inner)
    m_all[x, y, :, 128:] = (0.5 * pre * (1.0 + bend)).astype(BF16)

    class Spread:
        def __init__(self, a):
            self.a = a
            self.line, self.near, self.far = take(4), take(8), take(8)
            own = a.at[x, y]
            push(own, own, dp_at(x, lax.min(y + 1, 3)), when=y < 3, at=self.line + y)
            push(own, own, dp_at(x, lax.max(y - 1, 0)), when=y > 0, at=self.line + y)

        def along_y(self, s, then=None):
            for sign in (-1, 1):
                there = y + sign * s
                yy = lax.rem(there + 4, 4)
                here = (there >= 0) & (there < 4)
                block = self.a.at[x, yy]

                @pl.when(here)
                def _():
                    expect(block, self.line + yy)

                on = y - sign
                push(
                    block, block, dp_at(x, lax.clamp(0, on, 3)),
                    when=here & (on >= 0) & (on < 4), at=self.line + yy,
                )
                if then is not None:
                    then(yy, here)

        def send_near(self, yy, when=None):
            block = self.a.at[x, yy]
            push(block, block, x_right, when=when, at=self.near + yy)
            push(block, block, x_left, when=when, at=self.near + 4 + yy)

        def send_far(self, yy, when=None):
            first = self.a.at[around(x, 3), yy]
            second = self.a.at[around(x, 1), yy]

            def wait():
                expect(first, self.near + yy)
                expect(second, self.near + 4 + yy)

            if when is None:
                wait()
            else:
                pl.when(when)(wait)
            first, second = first.at[pl.ds(0, 64)], second.at[pl.ds(64, 64)]
            push(first, first, x_right, when=when, at=self.far + yy)
            push(second, second, x_left, when=when, at=self.far + 4 + yy)

        def far_step(self, s):
            for sign in (-1, 1):
                there = y + sign * s
                self.send_far(lax.rem(there + 4, 4), (there >= 0) & (there < 4))

        def ready(self, yy):
            far = self.a.at[around(x, 2), yy]
            expect(far.at[pl.ds(0, 64)], self.far + yy)
            expect(far.at[pl.ds(64, 64)], self.far + 4 + yy)

    ms = Spread(m_all)
    ms.send_near(y)
    slope = 0.5 * (1.0 + bend) + 0.5 * pre * (1.0 - bend * bend) * (
        GELU_ROOT * (1.0 + 3.0 * GELU_CUBE * (pre * pre))
    )
    gs.send_y(2)
    grad_mixed = gs.result()
    grad_attn = grad_mixed[:, :128].astype(BF16)
    r_all[x, y, :, 384:] = (grad_mixed[:, 128:] * slope).astype(BF16)
    dprob = mm_nt(grad_attn, value_b)
    delta = jnp.sum(prob * dprob, -1, keepdims=True)
    dscore = (prob * (dprob - delta)).astype(BF16)
    grad_qn = mm(dscore, key_b) * FACTOR
    grad_kn = mm_tn(dscore, query_b) * FACTOR
    r_all[x, y, :, :128] = head_back(grad_qn, query_unit, query_scale, qg).astype(BF16)
    r_all[x, y, :, 128:256] = head_back(grad_kn, key_unit, key_scale, kg).astype(BF16)
    r_all[x, y, :, 256:384] = mm_tn(prob_b, grad_attn).astype(BF16)
    rs = Spread(r_all)
    rs.send_near(y)
    ms.along_y(1, ms.send_near)
    ms.send_far(y)
    rs.along_y(1)
    ms.along_y(2, ms.send_near)
    ms.far_step(1)
    rs.along_y(2)
    ms.along_y(3, ms.send_near)
    ms.far_step(2)
    rs.send_near(2, y != 2)
    ms.far_step(3)
    rs.send_near(1, y != 1)

    class Reduce:
        def __init__(self, e, r, s, left, right, f, yv, got):
            self.e, self.r, self.s, self.left, self.right = e, r, s, left, right
            self.f, self.yv, self.got = f, yv, got
            self.core, self.ring = {}, None

        def chunk(self, yy, part):
            self.e[yy] = part.astype(BF16).reshape(4, 2, 64, FEATURES)
            self.core[yy] = [push(self.e.at[yy, :, 1 - c], self.r.at[yy], core_peer)]

        def core_sum(self, yy):
            arrive(self.core.pop(yy))
            own = self.e[yy, :, pl.ds(c, 1)].reshape(4, 64, FEATURES)
            total = (up(own) + up(self.r[yy])).astype(BF16)
            for xx in range(4):
                self.s[2 * yy + xx % 2, xx // 2] = total[xx]

        def step(self, s):
            if s == 1:
                first, second = pl.ds(0, 32), pl.ds(32, 32)
                self.ring = [
                    push(self.s.at[4, :, first], self.left.at[0, :, first], z_right),
                    push(self.s.at[4, :, second], self.right.at[0, :, second], z_left),
                ]
                return
            first, second = (slice(0, 32), slice(32, 64)) if s == 2 else (slice(None),) * 2
            a, b = self.ring
            arrive([a])
            new = up(self.s[5 - s, :, first]) + up(self.left[s - 2, :, first])
            self.s[5 - s, :, first] = new.astype(BF16)
            a = push(self.s.at[5 - s], self.left.at[s - 1], z_right)
            arrive([b])
            new = up(self.s[3 + s, :, second]) + up(self.right[s - 2, :, second])
            self.s[3 + s, :, second] = new.astype(BF16)
            b = push(self.s.at[3 + s], self.right.at[s - 1], z_left)
            self.ring = [a, b]

        def last(self):
            arrive(self.ring)
            self.f[...] = up(self.s[0]) + up(self.left[3]) + up(self.right[3])
            self.yv[...] = self.f[1 - h].astype(BF16)
            self.hi = [push(self.yv, self.got, hi_peer)]

        def result(self):
            arrive(self.hi)
            return self.f[h] + up(self.got[...])

    outs = Reduce(eo, reo, so, lo, ro, fo, yo, ryo)
    grads = Reduce(eg, reg, sg, lg, rg, fg, yg, ryg)

    def grad_product(yy):
        rs.ready(yy)
        grads.chunk(yy, mm_nt(r_all[:, yy].reshape(512, 768), bw[...]))

    def out_product(yy):
        ms.ready(yy)
        outs.chunk(yy, mm(m_all[:, yy].reshape(512, 512), ow[...]))

    out_product(2)
    rs.along_y(3)
    rs.send_near(3, y != 3)
    out_product(1)
    rs.send_far(2)
    outs.core_sum(2)
    outs.step(1)
    out_product(3)
    rs.send_near(0, y != 0)
    out_product(0)
    rs.send_far(1)
    outs.core_sum(1)
    outs.core_sum(3)
    outs.core_sum(0)
    outs.step(2)
    rs.send_far(3)
    grad_product(2)
    rs.send_far(0)
    grads.core_sum(2)
    grads.step(1)
    outs.step(3)
    grad_product(1)
    grads.core_sum(1)
    grads.step(2)
    outs.step(4)
    grad_product(3)
    grads.core_sum(3)
    grads.step(3)
    grad_product(0)
    grads.core_sum(0)
    grads.step(4)
    outs.last()
    weight = jnp.zeros((FEATURES, 768), F32)
    for yy in range(4):
        weight = weight + mm_tn(rows_of(nrm_all, yy), r_all[:, yy].reshape(512, 768))
    gwqkv_ref[...] = weight[:, :384].astype(BF16)
    gwin_ref[...] = weight[:, 384:].astype(BF16)
    grads.last()
    weight = jnp.zeros((512, FEATURES), F32)
    for yy in range(4):
        weight = weight + mm_tn(m_all[:, yy].reshape(512, 512), rows_of(cot_all, yy))
    gwo_ref[...] = weight[:128].astype(BF16)
    gwout_ref[...] = weight[128:].astype(BF16)
    out_ref[...] = (up(x_ref[...]) + outs.result()).astype(BF16)
    local_grad = grads.result() * gain
    centred = cen_ref[...]
    stats_b[x, y] = columns_to_rows(
        jnp.sum(local_grad, 1, keepdims=True),
        jnp.sum(local_grad * centred, 1, keepdims=True),
    )
    arrive(sums_x(stats_b))
    arrive(sums_y(stats_b))
    sums = jnp.sum(stats_b[...].reshape(16, 8, 128), 0) / D
    first, second = rows_to_columns(sums[0:1], sums[1:2])
    scaling = scl_ref[...][:, 0:1]
    gx_ref[...] = (
        up(cot_ref[...]) + scaling * (local_grad - first - centred * second)
    ).astype(BF16)
    for copy, when in started[-SENDS:]:
        finish(copy, when)


def place(*refs):
    n = len(refs) // 2
    for i in range(n):
        refs[n + i][...] = refs[i][...]


def shards(block_input, ln_gain, w_qkv, w_in, w_o, w_out, q_gain, k_gain, cotangent):
    def vmem(*shape):
        return pltpu.VMEM(shape, BF16)

    def scatter(cols):
        return [
            vmem(4, 4, 128, cols), vmem(4, 64, cols), vmem(4, 64, cols),
            vmem(4, 128, cols), vmem(4, 128, cols), vmem(4, 128, cols), vmem(4, 128, cols),
        ]

    ring = vmem(4, 2, 64, 384)
    scratch = [
        vmem(8, 2, 2, 64, 384), vmem(8, 2, 2, 64, 384), vmem(384, 768), vmem(512, 384),
        pltpu.VMEM((4, 4, 8, 128), F32), pltpu.VMEM((4, 4, 8, 128), F32),
        pltpu.VMEM((64, 384), F32), pltpu.VMEM((64, 128), F32),
        *scatter(512), *scatter(384), *scatter(384),
        vmem(4, 4, 128, 512), vmem(4, 4, 128, 768),
        vmem(4, 4, 2, 64, 384), vmem(4, 4, 2, 64, 384), vmem(4, 4, 64, 384), vmem(4, 4, 64, 384),
        vmem(8, 2, 64, 384), vmem(8, 2, 64, 384), ring, ring, ring, ring,
        pltpu.VMEM((2, 64, 384), F32), pltpu.VMEM((2, 64, 384), F32),
        vmem(64, 384), vmem(64, 384), vmem(64, 384), vmem(64, 384),
        pltpu.SemaphoreType.DMA((SENDS,)), pltpu.SemaphoreType.DMA((ARRIVALS,)),
    ]
    args = (block_input, cotangent, ln_gain, w_qkv, w_in, w_o, w_out, q_gain, k_gain)
    outs = (block_input, cotangent, w_qkv, w_in, w_o, w_out)
    shapes = tuple(jax.ShapeDtypeStruct(a.shape, BF16) for a in outs)
    results = pl.pallas_call(
        kernel,
        out_shape=shapes,
        in_specs=[pl.BlockSpec(memory_space=pltpu.VMEM)] * len(args),
        out_specs=tuple(pl.BlockSpec(memory_space=pltpu.VMEM) for _ in outs),
        scratch_shapes=scratch,
        compiler_params=pltpu.CompilerParams(
            collective_id=1, has_side_effects=True, vmem_limit_bytes=56 * 2**20
        ),
        name="block",
    )(*args)
    return pl.pallas_call(
        place,
        out_shape=shapes,
        in_specs=[pl.BlockSpec(memory_space=pltpu.VMEM)] * len(outs),
        out_specs=tuple(pl.BlockSpec(memory_space=pltpu.VMEM) for _ in outs),
        name="place",
    )(*results)


def solution(mesh):
    return jax.shard_map(
        shards,
        mesh=mesh,
        in_specs=(
            P("mp", "dp"),
            P("dp"),
            P("dp", "mp"),
            P("dp", "mp"),
            P("mp", "dp"),
            P("mp", "dp"),
            P("mp", None),
            P("mp", None),
            P("mp", "dp"),
        ),
        out_specs=(
            P("mp", "dp"),
            P("mp", "dp"),
            P("dp", "mp"),
            P("dp", "mp"),
            P("mp", "dp"),
            P("mp", "dp"),
        ),
        check_vma=False,
    )
```

```python
import math

import jax
import jax.numpy as jnp
from jax import lax
from jax.experimental import pallas as pl
from jax.experimental.pallas import tpu as pltpu
from jax.sharding import PartitionSpec as P

MESH = pl.DeviceIdType.MESH
D = 6144
FEATURES = 384
N_DP = 16
epsilon = 1e-06
F32 = jnp.float32
BF16 = jnp.bfloat16
FACTOR = 1.0 / math.sqrt(128)
GELU_ROOT = 0.7978845608028654
GELU_CUBE = 0.044715
NT = (((1,), (1,)), ((), ()))
TN = (((0,), (0,)), ((), ()))
SENDS = 32
ARRIVALS = 208
SCATTER_ORDER = (2, 1, 3, 0)


def mm(a, b):
    return jnp.dot(a, b, preferred_element_type=F32)


def mm_nt(a, b):
    return lax.dot_general(a, b, NT, preferred_element_type=F32)


def mm_tn(a, b):
    return lax.dot_general(a, b, TN, preferred_element_type=F32)


def up(v):
    return v.astype(F32)


def head_norm(values, gain):
    centre = values - jnp.mean(values, -1, keepdims=True)
    scaling = 1.0 / jnp.sqrt(jnp.mean(centre * centre, -1, keepdims=True) + epsilon)
    unit = centre * scaling
    return (unit * gain, unit, scaling)


def head_back(grad, unit, scaling, gain):
    local_grad = grad * gain
    return scaling * (
        local_grad
        - jnp.mean(local_grad, -1, keepdims=True)
        - unit * jnp.mean(local_grad * unit, -1, keepdims=True)
    )


def columns_to_rows(first, second):
    lane = lax.broadcasted_iota(jnp.int32, (64, 128), 1)
    block = jnp.where(lane == 0, first, jnp.where(lane == 1, second, 0.0))
    block = jnp.concatenate([block, jnp.zeros((64, 128), F32)], 0)
    return block.T[:8]


def rows_to_columns(first, second):
    row = lax.broadcasted_iota(jnp.int32, (128, 128), 0)
    block = jnp.where(row == 0, first, jnp.where(row == 1, second, 0.0)).T
    return block[:64, 0:1], block[:64, 1:2]


def kernel(
    x_ref, cot_ref, gain_ref, wqkv_ref, win_ref, wo_ref, wout_ref, qg_ref, kg_ref,
    out_ref, gx_ref, gwqkv_ref, gwin_ref, gwo_ref, gwout_ref,
    cot_all, nrm_all, bw, ow, stats, stats_b, cen_ref, scl_ref,
    g2, hl2, hr2, fl2, fr2, s2, t2,
    fp, hlf, hrf, flf, frf, sf, tf,
    ep, hle, hre, fle, fre, se, te,
    m_all, p_all, r_all, eo, eg, reo, reg, so, sg, lo, ro, lg, rg, fo, fg, yo, yg, ryo, ryg,
    send, recv, gates, own_sems,
):
    d = lax.axis_index("dp")
    m = lax.axis_index("mp")
    x, y = d // 4, lax.rem(d, 4)
    h, z, c = m // 16, lax.rem(m // 2, 8), lax.rem(m, 2)

    def dp_at(xx, yy):
        return (xx * 4 + yy, m)

    def around(v, o):
        return lax.rem(v + o, 4)

    x_peers = [dp_at(around(x, o), y) for o in (1, 2, 3)]
    y_peers = [dp_at(x, around(y, o)) for o in (1, 2, 3)]
    x_right, x_left = x_peers[0], x_peers[2]
    hi_peer = (d, (1 - h) * 16 + z * 2 + c)
    z_right = (d, h * 16 + lax.rem(z + 1, 8) * 2 + c)
    z_left = (d, h * 16 + lax.rem(z + 7, 8) * 2 + c)
    core_peer = (d, m + 1 - 2 * c)

    loads = [
        pltpu.make_async_copy(src, dst, own_sems.at[i])
        for i, (src, dst) in enumerate(
            (
                (wo_ref, ow.at[:128]), (wout_ref, ow.at[128:]),
                (wqkv_ref, bw.at[:, :384]), (win_ref, bw.at[:, 384:]),
            )
        )
    ]
    for load in loads:
        load.start()
    barrier = pltpu.get_barrier_semaphore()
    everyone = x_peers + y_peers + [hi_peer, z_right, z_left, core_peer]
    for peer in everyone:
        pl.semaphore_signal(barrier, inc=1, device_id=peer, device_id_type=MESH)

    started = []
    slots = []

    def take(n):
        first = len(slots)
        slots.extend([None] * n)
        return first

    def finish(copy, when):
        if when is None:
            copy.wait_send()
        else:
            pl.when(when)(copy.wait_send)

    def push(src, dst, peer, when=None, at=None):
        n = len(started)
        if n >= SENDS:
            finish(*started[n - SENDS])
        copy = pltpu.make_async_remote_copy(
            src_ref=src, dst_ref=dst, send_sem=send.at[n % SENDS],
            recv_sem=recv.at[take(1) if at is None else at],
            device_id=peer, device_id_type=MESH,
        )
        started.append((copy, when))
        if when is None:
            copy.start()
        else:
            pl.when(when)(copy.start)
        return copy

    def arrive(copies):
        for copy in copies:
            copy.wait_recv()

    def expect(dst, at):
        pltpu.make_async_remote_copy(
            src_ref=dst, dst_ref=dst, send_sem=send.at[0], recv_sem=recv.at[at],
            device_id=core_peer, device_id_type=MESH,
        ).wait_recv()

    gain = gain_ref[...][None, :]
    cot_all[z, h, c] = cot_ref[...]
    inputs = up(x_ref[...])
    local_mean = jnp.sum(inputs, 1, keepdims=True) / FEATURES
    local_centre = inputs - local_mean
    local_m2 = jnp.sum(local_centre * local_centre, 1, keepdims=True)
    stats[x, y] = columns_to_rows(local_mean, local_m2)
    pl.semaphore_wait(barrier, len(everyone))

    def hi_start(a):
        return [push(a.at[z, h, c], a.at[z, h, c], hi_peer)]

    def ring_start(a, kind, s):
        hh = h if kind == 0 else 1 - h
        right = lax.rem(z + 9 - s, 8)
        left = lax.rem(z + s - 1, 8)
        if s == 4:
            first, second = pl.ds(0, 32), pl.ds(32, 32)
            return [
                push(a.at[right, hh, c, first], a.at[right, hh, c, first], z_right),
                push(a.at[left, hh, c, second], a.at[left, hh, c, second], z_left),
            ]
        return [
            push(a.at[right, hh, c], a.at[right, hh, c], z_right),
            push(a.at[left, hh, c], a.at[left, hh, c], z_left),
        ]

    def core_start(a, s):
        ats = [z] if s == 0 else [lax.rem(z + s, 8)]
        if s in (1, 2, 3):
            ats.append(lax.rem(z + 8 - s, 8))
        return [push(a.at[at, :, c], a.at[at, :, c], core_peer) for at in ats]

    class Gather:
        def __init__(self, a):
            self.a = a
            self.hi = hi_start(a)
            self.own = ring_start(a, 0, 1)
            self.other = None
            self.core = {}

        def first_other(self):
            arrive(self.hi)
            self.other = ring_start(self.a, 1, 1)
            self.core[0] = core_start(self.a, 0)

        def own_step(self, s):
            arrive(self.own)
            self.own = ring_start(self.a, 0, s) if s < 5 else []

        def other_step(self, s):
            arrive(self.other)
            self.other = ring_start(self.a, 1, s) if s < 5 else []
            self.core[s - 1] = core_start(self.a, s - 1)

        def ready(self, s):
            arrive(self.core.pop(s))

    def rows_of(a, yy):
        parts = []
        for xx in range(4):
            at = lax.rem(z + 2 * yy + xx % 2, 8)
            parts.append(a[at, xx // 2].reshape(128, FEATURES))
        return jnp.concatenate(parts, 0)

    class Scatter:
        def __init__(self, part, hl, hr, fl, fr, s, t):
            self.part, self.hl, self.hr, self.fl, self.fr = part, hl, hr, fl, fr
            self.s, self.t = s, t
            self.base = take(4)
            self.half, self.full = {}, {}

        def send_half(self, yy):
            far = around(x, 2)
            first, second = pl.ds(0, 64), pl.ds(64, 64)
            self.half[yy] = [
                push(self.part.at[far, yy, first], self.hl.at[yy], x_right),
                push(self.part.at[far, yy, second], self.hr.at[yy], x_left),
            ]

        def send_full(self, yy):
            arrive(self.half.pop(yy))
            right, left = around(x, 1), around(x, 3)
            new = up(self.part[right, yy, :64]) + up(self.hl[yy])
            self.part[right, yy, :64] = new.astype(BF16)
            a = push(self.part.at[right, yy], self.fl.at[yy], x_right)
            new = up(self.part[left, yy, 64:]) + up(self.hr[yy])
            self.part[left, yy, 64:] = new.astype(BF16)
            b = push(self.part.at[left, yy], self.fr.at[yy], x_left)
            self.full[yy] = [a, b]

        def send_y(self, yy):
            arrive(self.full.pop(yy))
            total = up(self.part[x, yy]) + up(self.fl[yy]) + up(self.fr[yy])
            self.s[yy] = total.astype(BF16)
            o = lax.rem(yy - y + 4, 4)
            slot = lax.rem(o + 3, 4)
            push(
                self.s.at[yy], self.t.at[slot], dp_at(x, yy), when=o != 0, at=self.base + slot
            )

        def result(self):
            total = up(self.part[x, y]) + up(self.fl[y]) + up(self.fr[y])
            for i in range(3):
                expect(self.t.at[i], self.base + i)
                total = total + up(self.t[i])
            return total

    def sums_x(ref):
        return [push(ref.at[x, y], ref.at[x, y], peer) for peer in x_peers]

    def sums_y(ref):
        return [push(ref.at[:, y], ref.at[:, y], peer) for peer in y_peers]

    st = sums_x(stats)
    cg = Gather(cot_all)
    arrive(st)
    st = sums_y(stats)
    cg.first_other()
    cg.own_step(2)
    arrive(st)
    every = stats[...].reshape(16, 8, 128)
    mean_row = jnp.sum(every[:, 0:1, :], 0) / N_DP
    apart = every[:, 0:1, :] - mean_row[None]
    m2_row = jnp.sum(every[:, 1:2, :], 0) + FEATURES * jnp.sum(apart * apart, 0)
    scaling_row = 1.0 / jnp.sqrt(m2_row / D + epsilon)
    mean, scaling = rows_to_columns(mean_row, scaling_row)
    centred = (inputs - mean) * scaling
    nrm_all[z, h, c] = (centred * gain).astype(BF16)
    ng = Gather(nrm_all)
    cen_ref[...] = centred
    scl_ref[...] = jnp.broadcast_to(scaling, (64, 128))

    gs = Scatter(g2, hl2, hr2, fl2, fr2, s2, t2)
    fs = Scatter(fp, hlf, hrf, flf, frf, sf, tf)
    es = Scatter(ep, hle, hre, fle, fre, se, te)

    def g_product(yy):
        product = mm_nt(rows_of(cot_all, yy), ow[...]).astype(BF16)
        g2[:, yy] = product.reshape(4, 128, 512)
        gs.send_half(yy)

    def f_product(yy):
        product = mm(rows_of(nrm_all, yy), bw[...]).astype(BF16)
        fp[:, yy] = product[:, :384].reshape(4, 128, 384)
        fs.send_half(yy)
        ep[:, yy] = product[:, 384:].reshape(4, 128, 384)
        es.send_half(yy)

    cg.other_step(2)
    cg.own_step(3)
    ng.first_other()
    ng.own_step(2)
    cg.other_step(3)
    cg.own_step(4)
    cg.ready(0)
    cg.ready(1)
    for load in loads:
        load.wait()
    g_product(0)
    ng.other_step(2)
    ng.own_step(3)
    cg.other_step(4)
    cg.own_step(5)
    cg.ready(2)
    g_product(3)
    gs.send_full(0)
    ng.other_step(3)
    ng.own_step(4)
    cg.other_step(5)
    ng.ready(0)
    ng.ready(1)
    f_product(0)
    gs.send_full(3)
    gs.send_y(0)
    ng.other_step(4)
    ng.own_step(5)
    ng.ready(2)
    f_product(3)
    fs.send_full(0)
    es.send_full(0)
    ng.other_step(5)
    gs.send_y(3)
    ng.ready(3)
    f_product(1)
    fs.send_full(3)
    es.send_full(3)
    fs.send_y(0)
    ng.ready(4)
    f_product(2)
    es.send_y(0)
    fs.send_full(1)
    es.send_full(1)
    fs.send_y(3)
    cg.ready(3)
    cg.ready(4)
    g_product(1)
    fs.send_full(2)
    es.send_full(2)
    es.send_y(3)
    g_product(2)
    fs.send_y(1)
    es.send_y(1)
    gs.send_full(1)
    fs.send_y(2)
    es.send_y(2)
    gs.send_full(2)
    gs.send_y(1)
    qkv = fs.result()

    qg, kg = qg_ref[...], kg_ref[...]
    queries, query_unit, query_scale = head_norm(qkv[:, :128], qg)
    keys, key_unit, key_scale = head_norm(qkv[:, 128:256], kg)
    query_b, key_b = queries.astype(BF16), keys.astype(BF16)
    value_b = qkv[:, 256:].astype(BF16)
    expo = jnp.exp(mm_nt(query_b, key_b) * FACTOR)
    prob = expo / jnp.sum(expo, -1, keepdims=True)
    prob_b = prob.astype(BF16)
    m_all[x, y, :, :128] = mm(prob_b, value_b).astype(BF16)
    pre = es.result()
    inner = GELU_ROOT * (pre + GELU_CUBE * (pre * pre * pre))
    bend = jnp.tanh(inner)
    m_all[x, y, :, 128:] = (0.5 * pre * (1.0 + bend)).astype(BF16)

    class Spread:
        def __init__(self, a):
            self.a = a
            self.line, self.near, self.far = take(4), take(8), take(8)
            own = a.at[x, y]
            push(own, own, dp_at(x, lax.min(y + 1, 3)), when=y < 3, at=self.line + y)
            push(own, own, dp_at(x, lax.max(y - 1, 0)), when=y > 0, at=self.line + y)

        def along_y(self, s, then=None):
            for sign in (-1, 1):
                there = y + sign * s
                yy = lax.rem(there + 4, 4)
                here = (there >= 0) & (there < 4)
                block = self.a.at[x, yy]

                @pl.when(here)
                def _():
                    expect(block, self.line + yy)

                on = y - sign
                push(
                    block, block, dp_at(x, lax.clamp(0, on, 3)),
                    when=here & (on >= 0) & (on < 4), at=self.line + yy,
                )
                if then is not None:
                    then(yy, here)

        def send_near(self, yy, when=None):
            block = self.a.at[x, yy]
            push(block, block, x_right, when=when, at=self.near + yy)
            push(block, block, x_left, when=when, at=self.near + 4 + yy)

        def send_far(self, yy, when=None):
            first = self.a.at[around(x, 3), yy]
            second = self.a.at[around(x, 1), yy]

            def wait():
                expect(first, self.near + yy)
                expect(second, self.near + 4 + yy)

            if when is None:
                wait()
            else:
                pl.when(when)(wait)
            first, second = first.at[pl.ds(0, 64)], second.at[pl.ds(64, 64)]
            push(first, first, x_right, when=when, at=self.far + yy)
            push(second, second, x_left, when=when, at=self.far + 4 + yy)

        def far_step(self, s):
            for sign in (-1, 1):
                there = y + sign * s
                self.send_far(lax.rem(there + 4, 4), (there >= 0) & (there < 4))

        def ready(self, yy):
            far = self.a.at[around(x, 2), yy]
            expect(far.at[pl.ds(0, 64)], self.far + yy)
            expect(far.at[pl.ds(64, 64)], self.far + 4 + yy)

    ms = Spread(m_all)
    ms.send_near(y)
    slope = 0.5 * (1.0 + bend) + 0.5 * pre * (1.0 - bend * bend) * (
        GELU_ROOT * (1.0 + 3.0 * GELU_CUBE * (pre * pre))
    )
    gs.send_y(2)
    ms.along_y(1, ms.send_near)
    ms.send_far(y)
    grad_mixed = gs.result()
    grad_attn = grad_mixed[:, :128].astype(BF16)
    p_all[x, y] = (grad_mixed[:, 128:] * slope).astype(BF16)
    ps = Spread(p_all)
    ps.send_near(y)
    dprob = mm_nt(grad_attn, value_b)
    delta = jnp.sum(prob * dprob, -1, keepdims=True)
    dscore = (prob * (dprob - delta)).astype(BF16)
    grad_qn = mm(dscore, key_b) * FACTOR
    grad_kn = mm_tn(dscore, query_b) * FACTOR
    r_all[x, y, :, :128] = head_back(grad_qn, query_unit, query_scale, qg).astype(BF16)
    r_all[x, y, :, 128:256] = head_back(grad_kn, key_unit, key_scale, kg).astype(BF16)
    r_all[x, y, :, 256:] = mm_tn(prob_b, grad_attn).astype(BF16)
    rs = Spread(r_all)
    rs.send_near(y)
    ms.along_y(2, ms.send_near)
    ms.far_step(1)
    ps.along_y(1)
    rs.along_y(1)
    ms.along_y(3, ms.send_near)
    ms.far_step(2)
    ps.along_y(2)
    rs.along_y(2)
    ps.send_near(2, y != 2)
    rs.send_near(2, y != 2)
    ms.far_step(3)
    ps.send_near(1, y != 1)
    rs.send_near(1, y != 1)

    class Reduce:
        def __init__(self, e, r, s, left, right, f, yv, got):
            self.e, self.r, self.s, self.left, self.right = e, r, s, left, right
            self.f, self.yv, self.got = f, yv, got
            self.core, self.ring = {}, None

        def chunk(self, yy, part):
            self.e[yy] = part.astype(BF16).reshape(4, 2, 64, FEATURES)
            self.core[yy] = [push(self.e.at[yy, :, 1 - c], self.r.at[yy], core_peer)]

        def core_sum(self, yy):
            arrive(self.core.pop(yy))
            own = self.e[yy, :, pl.ds(c, 1)].reshape(4, 64, FEATURES)
            total = (up(own) + up(self.r[yy])).astype(BF16)
            for xx in range(4):
                self.s[2 * yy + xx % 2, xx // 2] = total[xx]

        def step(self, s):
            if s == 1:
                first, second = pl.ds(0, 32), pl.ds(32, 32)
                self.ring = [
                    push(self.s.at[4, :, first], self.left.at[0, :, first], z_right),
                    push(self.s.at[4, :, second], self.right.at[0, :, second], z_left),
                ]
                return
            first, second = (slice(0, 32), slice(32, 64)) if s == 2 else (slice(None),) * 2
            a, b = self.ring
            arrive([a])
            new = up(self.s[5 - s, :, first]) + up(self.left[s - 2, :, first])
            self.s[5 - s, :, first] = new.astype(BF16)
            a = push(self.s.at[5 - s], self.left.at[s - 1], z_right)
            arrive([b])
            new = up(self.s[3 + s, :, second]) + up(self.right[s - 2, :, second])
            self.s[3 + s, :, second] = new.astype(BF16)
            b = push(self.s.at[3 + s], self.right.at[s - 1], z_left)
            self.ring = [a, b]

        def last(self):
            arrive(self.ring)
            self.f[...] = up(self.s[0]) + up(self.left[3]) + up(self.right[3])
            self.yv[...] = self.f[1 - h].astype(BF16)
            self.hi = [push(self.yv, self.got, hi_peer)]

        def result(self):
            arrive(self.hi)
            return self.f[h] + up(self.got[...])

    outs = Reduce(eo, reo, so, lo, ro, fo, yo, ryo)
    grads = Reduce(eg, reg, sg, lg, rg, fg, yg, ryg)

    def grad_product(yy):
        ps.ready(yy)
        part = mm_nt(p_all[:, yy].reshape(512, 384), bw[:, 384:])
        rs.ready(yy)
        grads.chunk(yy, part + mm_nt(r_all[:, yy].reshape(512, 384), bw[:, :384]))

    def out_product(yy):
        ms.ready(yy)
        outs.chunk(yy, mm(m_all[:, yy].reshape(512, 512), ow[...]))

    out_product(2)
    ps.along_y(3)
    rs.along_y(3)
    ps.send_near(3, y != 3)
    rs.send_near(3, y != 3)
    out_product(1)
    ps.send_far(2)
    rs.send_far(2)
    ps.send_near(0, y != 0)
    rs.send_near(0, y != 0)
    outs.core_sum(2)
    outs.step(1)
    out_product(3)
    out_product(0)
    ps.send_far(1)
    rs.send_far(1)
    grad_product(2)
    outs.core_sum(1)
    outs.core_sum(3)
    outs.core_sum(0)
    ps.send_far(3)
    rs.send_far(3)
    grads.core_sum(2)
    grads.step(1)
    outs.step(2)
    grad_product(1)
    ps.send_far(0)
    rs.send_far(0)
    grads.core_sum(1)
    grads.step(2)
    outs.step(3)
    grad_product(3)
    grads.core_sum(3)
    grads.step(3)
    outs.step(4)
    grad_product(0)
    grads.core_sum(0)
    grads.step(4)
    outs.last()
    stores = []

    def store(rows, value, target):
        i = len(stores)
        gates[rows] = value.astype(BF16)
        copy = pltpu.make_async_copy(gates.at[rows], target, own_sems.at[4 + i])
        copy.start()
        stores.append(copy)

    for i, (source, target) in enumerate(((r_all, gwqkv_ref), (p_all, gwin_ref))):
        weight = jnp.zeros((FEATURES, 384), F32)
        for yy in range(4):
            weight = weight + mm_tn(rows_of(nrm_all, yy), source[:, yy].reshape(512, 384))
        store(pl.ds(384 * i, 384), weight, target)
    grads.last()
    weight = jnp.zeros((512, FEATURES), F32)
    for yy in range(4):
        weight = weight + mm_tn(m_all[:, yy].reshape(512, 512), rows_of(cot_all, yy))
    store(pl.ds(768, 128), weight[:128], gwo_ref)
    store(pl.ds(896, 384), weight[128:], gwout_ref)
    out_ref[...] = (up(x_ref[...]) + outs.result()).astype(BF16)
    local_grad = grads.result() * gain
    centred = cen_ref[...]
    stats_b[x, y] = columns_to_rows(
        jnp.sum(local_grad, 1, keepdims=True),
        jnp.sum(local_grad * centred, 1, keepdims=True),
    )
    arrive(sums_x(stats_b))
    arrive(sums_y(stats_b))
    sums = jnp.sum(stats_b[...].reshape(16, 8, 128), 0) / D
    first, second = rows_to_columns(sums[0:1], sums[1:2])
    scaling = scl_ref[...][:, 0:1]
    gx_ref[...] = (
        up(cot_ref[...]) + scaling * (local_grad - first - centred * second)
    ).astype(BF16)
    for copy in stores:
        copy.wait()
    for copy, when in started[-SENDS:]:
        finish(copy, when)


def place(*refs):
    n = len(refs) // 2
    for i in range(n):
        refs[n + i][...] = refs[i][...]


def shards(block_input, ln_gain, w_qkv, w_in, w_o, w_out, q_gain, k_gain, cotangent):
    def vmem(*shape):
        return pltpu.VMEM(shape, BF16)

    def scatter(cols):
        return [
            vmem(4, 4, 128, cols), vmem(4, 64, cols), vmem(4, 64, cols),
            vmem(4, 128, cols), vmem(4, 128, cols), vmem(4, 128, cols), vmem(4, 128, cols),
        ]

    ring = vmem(4, 2, 64, 384)
    scratch = [
        vmem(8, 2, 2, 64, 384), vmem(8, 2, 2, 64, 384), vmem(384, 768), vmem(512, 384),
        pltpu.VMEM((4, 4, 8, 128), F32), pltpu.VMEM((4, 4, 8, 128), F32),
        pltpu.VMEM((64, 384), F32), pltpu.VMEM((64, 128), F32),
        *scatter(512), *scatter(384), *scatter(384),
        vmem(4, 4, 128, 512), vmem(4, 4, 128, 384), vmem(4, 4, 128, 384),
        vmem(4, 4, 2, 64, 384), vmem(4, 4, 2, 64, 384), vmem(4, 4, 64, 384), vmem(4, 4, 64, 384),
        vmem(8, 2, 64, 384), vmem(8, 2, 64, 384), ring, ring, ring, ring,
        pltpu.VMEM((2, 64, 384), F32), pltpu.VMEM((2, 64, 384), F32),
        vmem(64, 384), vmem(64, 384), vmem(64, 384), vmem(64, 384),
        pltpu.SemaphoreType.DMA((SENDS,)), pltpu.SemaphoreType.DMA((ARRIVALS,)),
        vmem(1280, 384), pltpu.SemaphoreType.DMA((8,)),
    ]
    args = (block_input, cotangent, ln_gain, w_qkv, w_in, w_o, w_out, q_gain, k_gain)
    outs = (block_input, cotangent, w_qkv, w_in, w_o, w_out)
    shapes = tuple(jax.ShapeDtypeStruct(a.shape, BF16) for a in outs)
    results = pl.pallas_call(
        kernel,
        out_shape=shapes,
        in_specs=[pl.BlockSpec(memory_space=pl.ANY if 3 <= i < 7 else pltpu.VMEM) for i in range(9)],
        out_specs=tuple(
            pl.BlockSpec(memory_space=pltpu.VMEM if i < 2 else pl.ANY) for i in range(6)
        ),
        scratch_shapes=scratch,
        compiler_params=pltpu.CompilerParams(
            collective_id=1, has_side_effects=True, vmem_limit_bytes=56 * 2**20
        ),
        name="block",
    )(*args)
    return pl.pallas_call(
        place,
        out_shape=shapes,
        in_specs=[pl.BlockSpec(memory_space=pltpu.VMEM)] * len(outs),
        out_specs=tuple(pl.BlockSpec(memory_space=pltpu.VMEM) for _ in outs),
        name="place",
    )(*results)


def solution(mesh):
    return jax.shard_map(
        shards,
        mesh=mesh,
        in_specs=(
            P("mp", "dp"),
            P("dp"),
            P("dp", "mp"),
            P("dp", "mp"),
            P("mp", "dp"),
            P("mp", "dp"),
            P("mp", None),
            P("mp", None),
            P("mp", "dp"),
        ),
        out_specs=(
            P("mp", "dp"),
            P("mp", "dp"),
            P("dp", "mp"),
            P("dp", "mp"),
            P("mp", "dp"),
            P("mp", "dp"),
        ),
        check_vma=False,
    )
```
